32 devices in a mesh: span: 16 (over z, x, core), section: 2 (over y).
Axes of the slice: x: 2, y: 2, z: 4, core: 2. Of those that a mesh axis runs over, the one named last changes fastest.
Arguments:
- clip_tokens: bfloat16 [2176, 1120], P('span'), may hold values from -6 to 6
- frame_ids: int32 [2176], P('span'), may hold values from 0 to 63, never falling along the last dimension, each value on 1 to 68 neighbouring positions
- norm_gain: float32 [2, 1120], P('section'), may hold values from 0.25 to 1.75
- qkv_weight: bfloat16 [2, 3763200], P('section', 'span'), may hold values from -0.1875 to 0.1875
- head_gain: float32 [2, 1120], P('section'), may hold values from 0.25 to 1.75
- out_weight: bfloat16 [2, 1254400], P('section', 'span'), may hold values from -0.1875 to 0.1875
Outputs:
- section_outputs: bfloat16 [2, 2176, 1120], P('section', 'span')
The draws below stay inside these ranges and needn't reach their ends.
Inputs may be any that keep to these rules, and one draw needn't show every extreme that they name: `frame_ids`: frame numbers never fall along the clip.
All inputs are finite; a program needn't handle non-finite values.
Results may differ from the reference program's by a relative error of at most 0.0064.
Values may be sent and summed in bfloat16 or wider, within the bound.
A program may use at most 64 MiB of HBM per device.

```python
import math
import jax
import jax.numpy as jnp
import numpy as np
from jax import lax

D = 1120
HEADS = 10
HEAD = 112
ROWS = 136
FRAMES = 4
QKV = 3360
LAYERS = 2
TOKENS = 2176
N_SPAN = 16


def levels(key, shape, pieces, low, high):
    gain, own = 1.0, jax.random.fold_in(key, 6)
    for dim, parts in pieces:
        heights = jnp.exp(jax.random.uniform(jax.random.fold_in(own, dim), (parts,), jnp.float32, low / len(pieces), high / len(pieces)))
        gain = gain * jnp.repeat(heights, shape[dim] // parts).reshape([-1 if axis == dim else 1 for axis in range(len(shape))])
    return gain


def split_up(number_of, total, most, skew):
    loads = [(1 << 20) // math.isqrt(standing ** skew) + 1 for standing in range(2, number_of + 1)]
    rest, holding = total - most - (number_of - 1), [1] * (number_of - 1)
    while rest > 0:
        free = [i for i in range(number_of - 1) if holding[i] < most]
        pool, remaining = sum([loads[i] for i in free]), rest
        for i in free:
            more = min(most - holding[i], max(1, remaining * loads[i] // pool), rest)
            holding[i] = holding[i] + more
            rest = rest - more
    return np.array([most] + holding)


def uneven(own_key, amount, total, limit, lean):
    if amount == 2:
        one = jax.random.randint(own_key, (), max(1, total - limit), min(limit, total - 1) + 1)
        return jnp.stack([one, total - one])
    sizes = jnp.asarray(split_up(amount, total, limit, lean), jnp.int32)
    pairs = (amount - 1) // 2
    source_of, taker = sizes[1:1 + 2 * pairs:2], sizes[2:2 + 2 * pairs:2]
    room = jnp.minimum(source_of - 1, limit - taker)
    passed = jax.random.randint(jax.random.fold_in(own_key, 1), (pairs,), 0, 1 << 20) % (room + 1)
    sizes = sizes.at[1:1 + 2 * pairs:2].set(source_of - passed).at[2:2 + 2 * pairs:2].set(taker + passed)
    return sizes[jax.random.permutation(jax.random.fold_in(own_key, 2), amount)]


def scatter_about(key, dims, spread, reach, pieces=(), dtype=jnp.bfloat16):
    gain = levels(key, dims, pieces, -0.22, 0.18) if pieces else 1.0
    array = jax.random.normal(key, dims, jnp.float32) * spread * gain
    return jnp.minimum(jnp.maximum(array, -reach), reach).astype(dtype)


def setup_inputs(seed: int = 0) -> dict:
    key_of = jax.random.split(jax.random.key(seed), 7)
    clip_tokens = scatter_about(key_of[0], (TOKENS, D), 1.0, 6.0, ((0, 16),))
    frame_ids = jnp.searchsorted(jnp.cumsum(uneven(key_of[1], FRAMES * N_SPAN, TOKENS, ROWS // 2, 1)), jnp.arange(TOKENS), side="right").astype(jnp.int32)
    norm_gain = jnp.clip(1.0 + 0.15 * jax.random.normal(key_of[2], (LAYERS, D), jnp.float32), 0.25, 1.75)
    qkv_weight = scatter_about(key_of[3], (LAYERS, D * QKV), D ** -0.5, 0.1875, ((0, 2), (1, 16)))
    head_gain = jnp.clip(1.0 + 0.15 * jax.random.normal(key_of[4], (LAYERS, HEADS * HEAD), jnp.float32), 0.25, 1.75)
    out_weight = scatter_about(key_of[5], (LAYERS, HEADS * HEAD * D), (HEADS * HEAD) ** -0.5, 0.1875, ((0, 2), (1, 16)))
    return {"clip_tokens": clip_tokens, "frame_ids": frame_ids, "norm_gain": norm_gain, "qkv_weight": qkv_weight, "head_gain": head_gain, "out_weight": out_weight}


def one_layer(current, allowed, norm_scale, w_qkv, head_scale, w_out):
    inner_width = HEADS * HEAD
    current_wide = current.astype(jnp.float32)
    normed = (current_wide * lax.rsqrt(lax.optimization_barrier(jnp.mean(current_wide * current_wide, axis=1, keepdims=True)) + 1e-06) * norm_scale).astype(jnp.bfloat16)
    projected = jnp.dot(normed, w_qkv, preferred_element_type=jnp.float32)
    queries = jnp.maximum(projected[:, :inner_width], 0.0).astype(jnp.bfloat16)
    key_feats = jnp.maximum(projected[:, inner_width:2 * inner_width], 0.0).astype(jnp.bfloat16)
    value_rows = projected[:, 2 * inner_width:].astype(jnp.bfloat16)
    shape_four = (N_SPAN, ROWS, HEADS, HEAD)
    query_wide = queries.reshape(shape_four).astype(jnp.float32)
    key_wide = key_feats.reshape(shape_four).astype(jnp.float32)
    value_wide = value_rows.reshape(shape_four).astype(jnp.float32)
    span_state = jnp.einsum('cjhd,cjhe->chde', key_wide, value_wide)
    running_sum = jnp.cumsum(span_state, axis=0)
    carried = jnp.concatenate([jnp.zeros_like(span_state[:1]), running_sum[:-1]], axis=0).astype(jnp.bfloat16)
    scores = jnp.einsum('cihd,cjhd->chij', query_wide, key_wide)
    scores = jnp.where(allowed[:, None, :, :], scores, 0.0).astype(jnp.bfloat16)
    local_part = jnp.einsum('chij,cjhd->cihd', scores.astype(jnp.float32), value_wide)
    mixture = local_part + jnp.einsum('cihd,chde->cihe', query_wide, carried.astype(jnp.float32))
    attended = (mixture * lax.rsqrt(lax.optimization_barrier(jnp.mean(mixture * mixture, axis=3, keepdims=True)) + 1e-06) * head_scale.reshape(HEADS, HEAD)).astype(jnp.bfloat16)
    attended = attended.reshape(N_SPAN * ROWS, inner_width)
    return (current_wide + jnp.dot(attended, w_out, preferred_element_type=jnp.float32)).astype(jnp.bfloat16)

def reference(clip_tokens, frame_ids, norm_gain, qkv_weight, head_gain, out_weight):
    frames = frame_ids.reshape(N_SPAN, ROWS)
    allowed = frames[:, None, :] <= frames[:, :, None]
    current = clip_tokens
    collected = []
    for layer_index in range(LAYERS):
        w_qkv = qkv_weight[layer_index].reshape(D, 3 * HEADS * HEAD)
        w_out = out_weight[layer_index].reshape(HEADS * HEAD, D)
        current = one_layer(current, allowed, norm_gain[layer_index], w_qkv, head_gain[layer_index], w_out)
        collected.append(current)
    return jnp.stack(collected, axis=0)
```

```python
import jax
import jax.numpy as jnp
from jax import lax
from jax.experimental import pallas as pl
from jax.experimental.pallas import tpu as pltpu
from jax.sharding import PartitionSpec as P

HEAD = 112
LANES = 128
EPS = 1e-06


def shifted(block, axis, distance):
    devices = range(lax.axis_size(axis))
    route = [(i - distance, i) for i in devices if i - distance in devices]
    return lax.ppermute(block, axis, route)


def on_device(clip_tokens, frame_ids, norm_gain, qkv_weight, head_gain, out_weight):
    row_count = clip_tokens.shape[0]
    model_width = clip_tokens.shape[1]
    qkv_flat, out_flat = (
        lax.all_gather(qkv_weight, "span", axis=1, tiled=True),
        lax.all_gather(out_weight, "span", axis=1, tiled=True),
    )
    w_qkv = qkv_flat.reshape(model_width, -1)
    inner_width = w_qkv.shape[1] // 3
    w_out = out_flat.reshape(inner_width, model_width)
    head_count = inner_width // HEAD
    norm_scale = norm_gain[0]
    head_scale = head_gain[0].reshape(head_count, HEAD)
    allowed = frame_ids[None, :] <= frame_ids[:, None]
    section_count = lax.axis_size("section")
    span_count = lax.axis_size("span")
    my_section = lax.axis_index("section")

    def project(current):
        current_wide = current.astype(jnp.float32)
        normed = (
            current_wide
            * lax.rsqrt(jnp.mean(current_wide * current_wide, axis=1, keepdims=True) + 1e-06)
            * norm_scale
        ).astype(jnp.bfloat16)
        projected = jnp.dot(normed, w_qkv, preferred_element_type=jnp.float32)
        queries = (
            jnp.maximum(projected[:, :inner_width], 0.0)
            .astype(jnp.bfloat16)
            .reshape(row_count, head_count, HEAD)
        )
        key_feats = (
            jnp.maximum(projected[:, inner_width : 2 * inner_width], 0.0)
            .astype(jnp.bfloat16)
            .reshape(row_count, head_count, HEAD)
        )
        value_rows = (
            projected[:, 2 * inner_width :]
            .astype(jnp.bfloat16)
            .reshape(row_count, head_count, HEAD)
        )
        span_state = jnp.einsum(
            "jhd,jhe->hde", key_feats, value_rows, preferred_element_type=jnp.float32
        )
        return (queries, key_feats, value_rows, span_state)

    def local_term(queries, key_feats, value_rows):
        scores = jnp.einsum("ihd,jhd->hij", queries, key_feats, preferred_element_type=jnp.float32)
        weights = jnp.where(allowed[None, :, :], scores, 0.0).astype(jnp.bfloat16)
        return jnp.einsum("hij,jhd->ihd", weights, value_rows, preferred_element_type=jnp.float32)

    def finish(current, queries, local_part, carried):
        mixture = local_part + jnp.einsum(
            "ihd,hde->ihe", queries, carried, preferred_element_type=jnp.float32
        )
        attended = (
            mixture
            * lax.rsqrt(jnp.mean(mixture * mixture, axis=2, keepdims=True) + 1e-06)
            * head_scale
        ).astype(jnp.bfloat16)
        attended = attended.reshape(row_count, inner_width)
        return (
            current.astype(jnp.float32)
            + jnp.dot(attended, w_out, preferred_element_type=jnp.float32)
        ).astype(jnp.bfloat16)

    def prefix(span_state):
        sliced = span_state.reshape(span_count, -1)
        owned = lax.all_to_all(sliced, "span", split_axis=0, concat_axis=0, tiled=True)
        running = jnp.cumsum(owned, axis=0)
        earlier = (running - owned).astype(jnp.bfloat16)
        returned = lax.all_to_all(earlier, "span", split_axis=0, concat_axis=0, tiled=True)
        return returned.reshape(span_state.shape)

    empty_heads = jnp.zeros((row_count, head_count, HEAD), jnp.bfloat16)
    empty_state = jnp.zeros((head_count, HEAD, HEAD), jnp.float32)

    def step(step_index, loop_state):
        current, result = loop_state
        active = my_section == step_index

        def early_on(operand):
            return project(operand)

        def early_off(operand):
            return (empty_heads, empty_heads, empty_heads, empty_state)

        queries, key_feats, value_rows, span_state = lax.cond(active, early_on, early_off, current)
        carried = prefix(span_state)

        def late_on(operands):
            local_part = local_term(operands[1], operands[2], operands[3])
            return finish(operands[0], operands[1], local_part, operands[4])

        def late_off(operands):
            return jnp.zeros_like(operands[0])

        updated = lax.cond(
            active, late_on, late_off, (current, queries, key_feats, value_rows, carried)
        )
        result = jnp.where(active, updated, result)
        arrived = shifted(updated, "section", 1)
        return (arrived, result)

    initial = (clip_tokens, jnp.zeros_like(clip_tokens))
    final_state = lax.fori_loop(0, section_count, step, initial)
    return final_state[1][None, :, :]


def whole_tiles(count, tile):
    return -(-count // tile) * tile


def remote(src, dst, send, recv, span, section):
    return pltpu.make_async_remote_copy(
        src_ref=src,
        dst_ref=dst,
        send_sem=send,
        recv_sem=recv,
        device_id={"span": span, "section": section},
        device_id_type=pl.DeviceIdType.MESH,
    )


def spread(size_in, size_out, group_in, kept_in, group_out, kept_out):
    row = lax.broadcasted_iota(jnp.int32, (size_in, size_out), 0)
    col = lax.broadcasted_iota(jnp.int32, (size_in, size_out), 1)
    row_in, col_in = row % group_in, col % group_out
    row_feature = row // group_in * kept_in + row_in
    col_feature = col // group_out * kept_out + col_in
    same = (row_feature == col_feature) & (row_in < kept_in) & (col_in < kept_out)
    return jnp.where(same, 1.0, 0.0).astype(jnp.bfloat16)


def layers_kernel(
    x_ref, frame_ref, norm_ref, qkv_ref, head_ref, out_w_ref, y_ref,
    held, packed, stream, normed, queries, keys, values, mixed, attended, fresh,
    state, sent_state, got_state, sent_sum, got_sum,
    frames, masks, norm_scale, head_scale, to_shards, from_heads,
    gather_send, gather_recv, pair_send, pair_recv, state_send, state_recv,
    sum_send, sum_recv, y_send, y_recv, local_sem,
):
    f32, bf16 = jnp.float32, jnp.bfloat16
    span = lax.axis_index("span")
    section = lax.axis_index("section")
    core = span % 2
    chip = span // 2
    x_at = chip % 2
    z_at = chip // 2
    pair = span + 1 - 2 * core
    x_near = span + 2 - 4 * x_at
    chips = got_state.shape[0]
    z_count = chips // 2
    shards, shard_rows = held.shape[0], held.shape[1]
    rows = x_ref.shape[0]
    padded = stream.shape[1] // 2
    half_width = x_ref.shape[1] // 2
    half_lanes = stream.shape[2]
    heads = half_width // HEAD
    kept = qkv_ref.shape[0]
    width = 2 * half_width

    frames[...] = jnp.zeros_like(frames)
    frames[pl.ds(core, 1), 0:1, 0:rows] = frame_ref[...].astype(f32)[None]

    barrier = pltpu.get_barrier_semaphore()
    for step in range(1, chips):
        other = (chip + step) % chips * 2 + core
        pl.semaphore_signal(
            barrier, inc=1, device_id={"span": other, "section": section},
            device_id_type=pl.DeviceIdType.MESH,
        )
    pl.semaphore_signal(
        barrier, inc=1, device_id={"span": pair, "section": section},
        device_id_type=pl.DeviceIdType.MESH,
    )
    pl.semaphore_signal(
        barrier, inc=1, device_id={"span": span, "section": 1 - section},
        device_id_type=pl.DeviceIdType.MESH,
    )

    packed[...] = jnp.zeros_like(packed)
    for part in range(2):
        for third in range(3):
            for head in range(heads):
                at = third * width + part * half_width + head * HEAD
                to = (third * heads + head) * LANES
                packed[part, 0:kept, to : to + HEAD] = qkv_ref[:, at : at + HEAD]
        to = 3 * heads * LANES
        packed[part, 0:kept, to : to + half_width] = out_w_ref[
            :, part * half_width : (part + 1) * half_width
        ]

    pl.semaphore_wait(barrier, chips + 1)

    own = pltpu.make_async_copy(packed.at[core], held.at[span], local_sem)
    own.start()
    give = remote(packed.at[1 - core], held.at[span], pair_send.at[0], gather_recv.at[span], pair, section)
    give.start()
    give_frames = remote(frames.at[core], frames.at[core], pair_send.at[1], pair_recv.at[1], pair, section)
    give_frames.start()
    own.wait()

    def forward(lane, shard, target):
        return remote(
            held.at[shard], held.at[shard], gather_send.at[lane, shard], gather_recv.at[shard],
            target, section,
        )

    def arrival(shard):
        return remote(
            held.at[shard], held.at[shard], gather_send.at[0, shard], gather_recv.at[shard],
            pair, section,
        )

    def pass_on(step, from_core, first):
        if step == 0:
            shard = z_at * 4 + x_at * 2 + from_core
            if not first:
                arrival(shard).wait_recv()

            @pl.when(z_at < z_count - 1)
            def _():
                forward(0, shard, span + 4).start()

            @pl.when(z_at > 0)
            def _():
                forward(1, shard, span - 4).start()

            forward(2, shard, x_near).start()
        else:
            below = (z_at - step) * 4 + x_at * 2 + from_core
            above = (z_at + step) * 4 + x_at * 2 + from_core

            @pl.when(z_at >= step)
            def _():
                arrival(below).wait_recv()

                @pl.when(z_at < z_count - 1)
                def _():
                    forward(0, below, span + 4).start()

                forward(2, below, x_near).start()

            @pl.when(z_at + step < z_count)
            def _():
                arrival(above).wait_recv()

                @pl.when(z_at > 0)
                def _():
                    forward(1, above, span - 4).start()

                forward(2, above, x_near).start()

    pass_on(0, core, True)
    pass_on(0, 1 - core, False)

    to_shards[...] = spread(half_lanes, half_lanes, half_lanes, half_width, shard_rows, kept)
    from_heads[...] = spread(half_lanes, half_lanes, LANES, HEAD, shard_rows, kept)
    norm_scale[...] = jnp.zeros_like(norm_scale)
    for part in range(2):
        norm_scale[part : part + 1, 0:half_width] = norm_ref[
            :, part * half_width : (part + 1) * half_width
        ]
    head_scale[...] = jnp.zeros_like(head_scale)
    for head in range(2 * heads):
        head_scale[head : head + 1, 0:HEAD] = head_ref[:, head * HEAD : (head + 1) * HEAD]
    give_frames.wait()
    eye = lax.broadcasted_iota(jnp.int32, (padded, padded), 0) == lax.broadcasted_iota(
        jnp.int32, (padded, padded), 1
    )
    for which in range(2):
        along = jnp.broadcast_to(frames[which, 0:1, 0:padded], (padded, padded))
        down = jnp.sum(jnp.where(eye, along, 0.0), axis=1, keepdims=True)
        masks[which] = jnp.where(along <= down, 1.0, 0.0)

    mine = pl.ds(pl.multiple_of(core * padded, 16), padded)
    theirs = pl.ds(pl.multiple_of((1 - core) * padded, 16), padded)

    @pl.when(section == 0)
    def _():
        fresh[...] = jnp.zeros_like(fresh)
        for part in range(2):
            fresh[part, 0:rows, 0:half_width] = x_ref[
                :, part * half_width : (part + 1) * half_width
            ]
        put = pltpu.make_async_copy(fresh, stream.at[:, mine, :], local_sem)
        put.start()
        share = remote(fresh, stream.at[:, mine, :], pair_send.at[2], pair_recv.at[2], pair, section)
        share.start()
        put.wait()
        share.wait()

    for step in range(1, z_count):
        pass_on(step, core, False)
        pass_on(step, 1 - core, False)

    for z_from in range(z_count):
        for from_core in range(2):
            arrival(z_from * 4 + (1 - x_at) * 2 + from_core).wait_recv()

    @pl.when(section == 1)
    def _():
        arrive = remote(
            stream.at[core], stream.at[core], y_send, y_recv, span, 1 - section
        )
        arrive.wait_recv()
        share = remote(
            stream.at[core], stream.at[core], pair_send.at[2], pair_recv.at[2], pair, section
        )
        share.start()
        share.wait()

    wide = [stream[part].astype(f32) for part in range(2)]
    square = sum(jnp.sum(value * value, axis=1, keepdims=True) for value in wide)
    inverse = lax.rsqrt(square / width + EPS)
    for part in range(2):
        scaled = (wide[part] * inverse * norm_scale[part : part + 1, :]).astype(bf16)
        normed[:, part * half_lanes : (part + 1) * half_lanes] = jnp.dot(
            scaled, to_shards[...], preferred_element_type=f32
        ).astype(bf16)
    lanes = heads * LANES
    depth = shards * shard_rows
    for third, into in ((1, keys), (2, values), (0, queries)):
        weight = held[:, :, third * lanes : (third + 1) * lanes].reshape(depth, lanes)
        result = jnp.dot(normed[...], weight, preferred_element_type=f32)
        into[...] = (result if third == 2 else jnp.maximum(result, 0.0)).astype(bf16)

    contract_rows = (((0,), (0,)), ((), ()))
    for which in range(2):
        at = slice(which * padded, (which + 1) * padded)
        for head in range(heads):
            cols = slice(head * LANES, (head + 1) * LANES)
            state[which, cols, :] = lax.dot_general(
                keys[at, cols], values[at, cols], contract_rows, preferred_element_type=f32
            )
    piece = sent_state.shape[1]
    sent_state[...] = (state[0] + state[1]).astype(bf16).reshape(chips, piece, LANES)

    def exchange(source, target, sends, recvs, step):
        other = (chip + step) % chips
        return remote(
            source.at[other], target.at[chip], sends.at[other], recvs.at[chip],
            other * 2 + core, section,
        )

    def landed(target, sends, recvs, step):
        other = (chip + step) % chips
        return remote(
            target.at[other], target.at[other], sends.at[other], recvs.at[other],
            other * 2 + core, section,
        )

    for step in range(1, chips):
        exchange(sent_state, got_state, state_send, state_recv, step).start()
    got_state[pl.ds(chip, 1)] = sent_state[pl.ds(chip, 1)]

    contract_lanes = (((1,), (1,)), ((), ()))

    def local_part(which):
        at = slice(which * padded, (which + 1) * padded)
        for head in range(heads):
            cols = slice(head * LANES, (head + 1) * LANES)
            scores = lax.dot_general(
                queries[at, cols], keys[at, cols], contract_lanes, preferred_element_type=f32
            )
            scores = jnp.where(masks[which] > 0.5, scores, 0.0).astype(bf16)
            mixed[at, cols] = jnp.dot(scores, values[at, cols], preferred_element_type=f32)

    local_part(0)
    for step in range(1, chips):
        landed(got_state, state_send, state_recv, step).wait_recv()
    running = jnp.zeros((piece, LANES), f32)
    for index in range(chips):
        sent_sum[index] = running.astype(bf16)
        running = running + got_state[index].astype(f32)
    for step in range(1, chips):
        exchange(sent_sum, got_sum, sum_send, sum_recv, step).start()
    got_sum[pl.ds(chip, 1)] = sent_sum[pl.ds(chip, 1)]
    local_part(1)
    for step in range(1, chips):
        landed(got_sum, sum_send, sum_recv, step).wait_recv()

    carried = got_sum[...].reshape(lanes, LANES)
    for which in range(2):
        at = slice(which * padded, (which + 1) * padded)
        for head in range(heads):
            cols = slice(head * LANES, (head + 1) * LANES)
            earlier = carried[cols, :]
            if which == 1:
                earlier = (earlier.astype(f32) + state[0, cols, :]).astype(bf16)
            mixture = mixed[at, cols] + jnp.dot(
                queries[at, cols], earlier, preferred_element_type=f32
            )
            size = jnp.sum(mixture * mixture, axis=1, keepdims=True) / HEAD
            queries[at, cols] = (
                mixture * lax.rsqrt(size + EPS) * head_scale[pl.ds(core * heads + head, 1), :]
            ).astype(bf16)
    fresh_heads = jnp.dot(queries[...], from_heads[...], preferred_element_type=f32)
    attended[pl.ds(core, 1)] = fresh_heads.astype(bf16)[None]
    swap = remote(attended.at[core], attended.at[core], pair_send.at[3], pair_recv.at[3], pair, section)
    swap.start()
    swap.wait()

    half_depth = depth // 2
    total = stream[pl.ds(core, 1)].astype(f32)[0]
    for part in range(2):
        weight = held[
            part * (shards // 2) : (part + 1) * (shards // 2), :, 3 * lanes : 3 * lanes + half_lanes
        ].reshape(half_depth, half_lanes)
        total = total + jnp.dot(attended[part], weight, preferred_element_type=f32)
    mixed_out = total.astype(bf16)
    keys[...] = mixed_out

    @pl.when(section == 0)
    def _():
        remote(keys, stream.at[core], y_send, y_recv, span, 1 - section).start()

    back = remote(keys.at[theirs, :], y_ref.at[core], pair_send.at[4], pair_recv.at[4], pair, section)
    back.start()
    keep = pltpu.make_async_copy(keys.at[mine, :], y_ref.at[core], local_sem)
    keep.start()
    keep.wait()
    back.wait()

    @pl.when(section == 0)
    def _():
        remote(keys, stream.at[core], y_send, y_recv, span, 1 - section).wait_send()

    give.wait_send()
    for step in range(1, chips):
        exchange(sent_state, got_state, state_send, state_recv, step).wait_send()
        exchange(sent_sum, got_sum, sum_send, sum_recv, step).wait_send()
    for z_from in range(z_count):
        for from_core in range(2):
            shard = z_from * 4 + x_at * 2 + from_core
            forward(2, shard, x_near).wait_send()

            @pl.when((z_from <= z_at) & (z_at < z_count - 1))
            def _():
                forward(0, shard, span + 4).wait_send()

            @pl.when((z_from >= z_at) & (z_at > 0))
            def _():
                forward(1, shard, span - 4).wait_send()


def fused(clip_tokens, frame_ids, norm_gain, qkv_weight, head_gain, out_weight):
    shards = lax.axis_size("span")
    rows, width = clip_tokens.shape
    half_width = width // 2
    kept = width // shards
    heads = half_width // HEAD
    shard_rows = whole_tiles(kept, 16)
    padded = whole_tiles(rows, 16)
    half_lanes = whole_tiles(half_width, LANES)
    lanes = heads * LANES
    chips = shards // 2
    bf16, f32 = jnp.bfloat16, jnp.float32
    dma = pltpu.SemaphoreType.DMA
    vmem = pl.BlockSpec(memory_space=pltpu.VMEM)
    y = pl.pallas_call(
        layers_kernel,
        out_shape=jax.ShapeDtypeStruct((2, padded, half_lanes), bf16),
        in_specs=[vmem] * 6,
        out_specs=vmem,
        scratch_shapes=[
            pltpu.VMEM((shards, shard_rows, 3 * lanes + half_lanes), bf16),
            pltpu.VMEM((2, shard_rows, 3 * lanes + half_lanes), bf16),
            pltpu.VMEM((2, 2 * padded, half_lanes), bf16),
            pltpu.VMEM((2 * padded, shards * shard_rows), bf16),
            pltpu.VMEM((2 * padded, lanes), bf16),
            pltpu.VMEM((2 * padded, lanes), bf16),
            pltpu.VMEM((2 * padded, lanes), bf16),
            pltpu.VMEM((2 * padded, lanes), f32),
            pltpu.VMEM((2, 2 * padded, half_lanes), bf16),
            pltpu.VMEM((2, padded, half_lanes), bf16),
            pltpu.VMEM((2, lanes, LANES), f32),
            pltpu.VMEM((chips, lanes // chips, LANES), bf16),
            pltpu.VMEM((chips, lanes // chips, LANES), bf16),
            pltpu.VMEM((chips, lanes // chips, LANES), bf16),
            pltpu.VMEM((chips, lanes // chips, LANES), bf16),
            pltpu.VMEM((2, 8, whole_tiles(padded, LANES)), f32),
            pltpu.VMEM((2, padded, padded), f32),
            pltpu.VMEM((8, half_lanes), f32),
            pltpu.VMEM((whole_tiles(2 * heads, 8), LANES), f32),
            pltpu.VMEM((half_lanes, half_lanes), bf16),
            pltpu.VMEM((lanes, half_lanes), bf16),
            dma((3, shards)),
            dma((shards,)),
            dma((5,)),
            dma((5,)),
            dma((chips,)),
            dma((chips,)),
            dma((chips,)),
            dma((chips,)),
            dma,
            dma,
            dma,
        ],
        compiler_params=pltpu.CompilerParams(
            collective_id=0, has_side_effects=True, vmem_limit_bytes=48 * 1024 * 1024
        ),
    )(
        clip_tokens,
        frame_ids.reshape(1, rows),
        norm_gain,
        qkv_weight.reshape(kept, -1),
        head_gain,
        out_weight.reshape(kept, width),
    )
    halves = y[:, :rows, :half_width]
    return jnp.concatenate([halves[0], halves[1]], axis=1)[None]


def grid_fits(mesh):
    return mesh.shape["span"] == 16 and mesh.shape["section"] == 2


def solution(mesh):
    return jax.shard_map(
        fused if grid_fits(mesh) else on_device,
        mesh=mesh,
        in_specs=(
            P("span", None),
            P("span"),
            P("section", None),
            P("section", "span"),
            P("section", None),
            P("section", "span"),
        ),
        out_specs=P("section", "span", None),
        check_vma=False,
    )
```

```python
import jax
import jax.numpy as jnp
from jax import lax
from jax.experimental import pallas as pl
from jax.experimental.pallas import tpu as pltpu
from jax.sharding import PartitionSpec as P

HEAD = 112
LANES = 128
EPS = 1e-06


def shifted(block, axis, distance):
    devices = range(lax.axis_size(axis))
    route = [(i - distance, i) for i in devices if i - distance in devices]
    return lax.ppermute(block, axis, route)


def on_device(clip_tokens, frame_ids, norm_gain, qkv_weight, head_gain, out_weight):
    row_count = clip_tokens.shape[0]
    model_width = clip_tokens.shape[1]
    qkv_flat, out_flat = (
        lax.all_gather(qkv_weight, "span", axis=1, tiled=True),
        lax.all_gather(out_weight, "span", axis=1, tiled=True),
    )
    w_qkv = qkv_flat.reshape(model_width, -1)
    inner_width = w_qkv.shape[1] // 3
    w_out = out_flat.reshape(inner_width, model_width)
    head_count = inner_width // HEAD
    norm_scale = norm_gain[0]
    head_scale = head_gain[0].reshape(head_count, HEAD)
    allowed = frame_ids[None, :] <= frame_ids[:, None]
    section_count = lax.axis_size("section")
    span_count = lax.axis_size("span")
    my_section = lax.axis_index("section")

    def project(current):
        current_wide = current.astype(jnp.float32)
        normed = (
            current_wide
            * lax.rsqrt(jnp.mean(current_wide * current_wide, axis=1, keepdims=True) + 1e-06)
            * norm_scale
        ).astype(jnp.bfloat16)
        projected = jnp.dot(normed, w_qkv, preferred_element_type=jnp.float32)
        queries = (
            jnp.maximum(projected[:, :inner_width], 0.0)
            .astype(jnp.bfloat16)
            .reshape(row_count, head_count, HEAD)
        )
        key_feats = (
            jnp.maximum(projected[:, inner_width : 2 * inner_width], 0.0)
            .astype(jnp.bfloat16)
            .reshape(row_count, head_count, HEAD)
        )
        value_rows = (
            projected[:, 2 * inner_width :]
            .astype(jnp.bfloat16)
            .reshape(row_count, head_count, HEAD)
        )
        span_state = jnp.einsum(
            "jhd,jhe->hde", key_feats, value_rows, preferred_element_type=jnp.float32
        )
        return (queries, key_feats, value_rows, span_state)

    def local_term(queries, key_feats, value_rows):
        scores = jnp.einsum("ihd,jhd->hij", queries, key_feats, preferred_element_type=jnp.float32)
        weights = jnp.where(allowed[None, :, :], scores, 0.0).astype(jnp.bfloat16)
        return jnp.einsum("hij,jhd->ihd", weights, value_rows, preferred_element_type=jnp.float32)

    def finish(current, queries, local_part, carried):
        mixture = local_part + jnp.einsum(
            "ihd,hde->ihe", queries, carried, preferred_element_type=jnp.float32
        )
        attended = (
            mixture
            * lax.rsqrt(jnp.mean(mixture * mixture, axis=2, keepdims=True) + 1e-06)
            * head_scale
        ).astype(jnp.bfloat16)
        attended = attended.reshape(row_count, inner_width)
        return (
            current.astype(jnp.float32)
            + jnp.dot(attended, w_out, preferred_element_type=jnp.float32)
        ).astype(jnp.bfloat16)

    def prefix(span_state):
        sliced = span_state.reshape(span_count, -1)
        owned = lax.all_to_all(sliced, "span", split_axis=0, concat_axis=0, tiled=True)
        running = jnp.cumsum(owned, axis=0)
        earlier = (running - owned).astype(jnp.bfloat16)
        returned = lax.all_to_all(earlier, "span", split_axis=0, concat_axis=0, tiled=True)
        return returned.reshape(span_state.shape)

    empty_heads = jnp.zeros((row_count, head_count, HEAD), jnp.bfloat16)
    empty_state = jnp.zeros((head_count, HEAD, HEAD), jnp.float32)

    def step(step_index, loop_state):
        current, result = loop_state
        active = my_section == step_index

        def early_on(operand):
            return project(operand)

        def early_off(operand):
            return (empty_heads, empty_heads, empty_heads, empty_state)

        queries, key_feats, value_rows, span_state = lax.cond(active, early_on, early_off, current)
        carried = prefix(span_state)

        def late_on(operands):
            local_part = local_term(operands[1], operands[2], operands[3])
            return finish(operands[0], operands[1], local_part, operands[4])

        def late_off(operands):
            return jnp.zeros_like(operands[0])

        updated = lax.cond(
            active, late_on, late_off, (current, queries, key_feats, value_rows, carried)
        )
        result = jnp.where(active, updated, result)
        arrived = shifted(updated, "section", 1)
        return (arrived, result)

    initial = (clip_tokens, jnp.zeros_like(clip_tokens))
    final_state = lax.fori_loop(0, section_count, step, initial)
    return final_state[1][None, :, :]


def whole_tiles(count, tile):
    return -(-count // tile) * tile


def remote(src, dst, send, recv, span, section):
    return pltpu.make_async_remote_copy(
        src_ref=src,
        dst_ref=dst,
        send_sem=send,
        recv_sem=recv,
        device_id={"span": span, "section": section},
        device_id_type=pl.DeviceIdType.MESH,
    )


def spread(size_in, size_out, group_in, kept_in, group_out, kept_out, skipped=0):
    row = lax.broadcasted_iota(jnp.int32, (size_in, size_out), 0) + (group_in - skipped)
    col = lax.broadcasted_iota(jnp.int32, (size_in, size_out), 1)
    row_in, col_in = row % group_in, col % group_out
    row_feature = (row // group_in - 1) * kept_in + row_in
    col_feature = col // group_out * kept_out + col_in
    same = (row_feature == col_feature) & (row_in < kept_in) & (col_in < kept_out)
    return jnp.where(same, 1.0, 0.0).astype(jnp.bfloat16)


def layers_kernel(
    x_ref, frame_ref, norm_ref, qkv_ref, head_ref, out_w_ref, y_ref,
    held_a, held_b, held_out, packed, packed_out, got, got_out, stream, normed, projected, queries, keys, values, mixed, attended, fresh,
    state, sent_state, got_state, sent_sum, got_sum,
    frames, masks, norm_scale, head_scale, to_blocks, from_heads, to_heads,
    gather_send, gather_recv, pair_send, pair_recv, state_send, state_recv,
    sum_send, sum_recv, y_send, y_recv, local_sem,
):
    f32, bf16 = jnp.float32, jnp.bfloat16
    span = lax.axis_index("span")
    section = lax.axis_index("section")
    core = span % 2
    chip = span // 2
    x_at = chip % 2
    z_at = chip // 2
    pair = span + 1 - 2 * core
    x_near = span + 2 - 4 * x_at
    chips = got_state.shape[0]
    z_count = chips // 2
    block_rows = held_a.shape[1]
    cut_at, window = held_a.shape[2], to_heads.shape[1]
    rows = x_ref.shape[0]
    padded = stream.shape[1] // 2
    half_width = x_ref.shape[1] // 2
    half_lanes = stream.shape[2]
    heads = half_width // HEAD
    kept = qkv_ref.shape[0]
    width = 2 * half_width

    frames[...] = jnp.zeros_like(frames)
    frames[pl.ds(core, 1), 0:1, 0:rows] = frame_ref[...].astype(f32)[None]

    barrier = pltpu.get_barrier_semaphore()
    for step in range(1, chips):
        other = (chip + step) % chips * 2 + core
        pl.semaphore_signal(
            barrier, inc=1, device_id={"span": other, "section": section},
            device_id_type=pl.DeviceIdType.MESH,
        )
    pl.semaphore_signal(
        barrier, inc=1, device_id={"span": pair, "section": section},
        device_id_type=pl.DeviceIdType.MESH,
    )
    pl.semaphore_signal(
        barrier, inc=1, device_id={"span": span, "section": 1 - section},
        device_id_type=pl.DeviceIdType.MESH,
    )

    packed[...] = jnp.zeros_like(packed)
    packed_out[...] = jnp.zeros_like(packed_out)
    for part in range(2):
        for third in range(3):
            at = third * width + part * half_width
            to = third * half_width
            packed[part, 0:kept, to : to + half_width] = qkv_ref[:, at : at + half_width]
        packed_out[part, 0:kept, 0:half_width] = out_w_ref[
            :, part * half_width : (part + 1) * half_width
        ]

    pl.semaphore_wait(barrier, chips + 1)

    give = remote(packed.at[1 - core], got, pair_send.at[0], pair_recv.at[0], pair, section)
    give.start()
    give_out = remote(packed_out.at[1 - core], got_out, pair_send.at[5], pair_recv.at[5], pair, section)
    give_out.start()
    give_frames = remote(frames.at[core], frames.at[core], pair_send.at[1], pair_recv.at[1], pair, section)
    give_frames.start()

    here = pl.ds(chip, 1)
    pieces = (held_a, held_b, held_out)
    for piece_ref in pieces:
        piece_ref[here, 2 * kept : block_rows, :] = jnp.zeros(
            (1, block_rows - 2 * kept, piece_ref.shape[2]), bf16
        )
    give.wait_recv()
    for which in range(2):

        @pl.when(core == which)
        def _():
            a, b = slice(which * kept, (which + 1) * kept), slice((1 - which) * kept, (2 - which) * kept)
            held_a[here, a, :] = packed[which, 0:kept, 0:cut_at][None]
            held_a[here, b, :] = got[0:kept, 0:cut_at][None]
            held_b[here, a, :] = packed[which, 0:kept, cut_at:][None]
            held_b[here, b, :] = got[0:kept, cut_at:][None]

    def forward(piece, lane, block, target):
        return remote(
            pieces[piece].at[block], pieces[piece].at[block],
            gather_send.at[piece * 3 + lane, block], gather_recv.at[piece, block],
            target, section,
        )

    def pass_on(piece, step):
        if step == 0:

            @pl.when(z_at < z_count - 1)
            def _():
                forward(piece, 0, chip, span + 4).start()

            @pl.when(z_at > 0)
            def _():
                forward(piece, 1, chip, span - 4).start()

            forward(piece, 2, chip, x_near).start()
        else:
            below = (z_at - step) * 2 + x_at
            above = (z_at + step) * 2 + x_at

            @pl.when(z_at >= step)
            def _():
                forward(piece, 2, below, x_near).wait_recv()

                @pl.when(z_at < z_count - 1)
                def _():
                    forward(piece, 0, below, span + 4).start()

                forward(piece, 2, below, x_near).start()

            @pl.when(z_at + step < z_count)
            def _():
                forward(piece, 2, above, x_near).wait_recv()

                @pl.when(z_at > 0)
                def _():
                    forward(piece, 1, above, span - 4).start()

                forward(piece, 2, above, x_near).start()

    def last_arrivals(piece):
        for z_from in range(z_count):
            forward(piece, 2, z_from * 2 + (1 - x_at), x_near).wait_recv()

    pass_on(0, 0)
    pass_on(1, 0)

    give_out.wait_recv()
    for which in range(2):

        @pl.when(core == which)
        def _():
            a, b = slice(which * kept, (which + 1) * kept), slice((1 - which) * kept, (2 - which) * kept)
            held_out[here, a, :] = packed_out[which, 0:kept, :][None]
            held_out[here, b, :] = got_out[0:kept, :][None]

    block_lanes = normed.shape[2]
    to_blocks[...] = spread(half_lanes, block_lanes, half_lanes, half_width, block_rows, 2 * kept)
    from_heads[...] = spread(heads * LANES, block_lanes, LANES, HEAD, block_rows, 2 * kept)
    window_at = [third * half_width // LANES * LANES for third in range(3)]
    for third in range(3):
        to_heads[third] = spread(
            window, heads * LANES, window, half_width, LANES, HEAD, third * half_width - window_at[third]
        )
    norm_scale[...] = jnp.zeros_like(norm_scale)
    for part in range(2):
        norm_scale[part : part + 1, 0:half_width] = norm_ref[
            :, part * half_width : (part + 1) * half_width
        ]
    head_scale[...] = jnp.zeros_like(head_scale)
    for head in range(2 * heads):
        head_scale[head : head + 1, 0:HEAD] = head_ref[:, head * HEAD : (head + 1) * HEAD]
    give_frames.wait()
    eye = lax.broadcasted_iota(jnp.int32, (padded, padded), 0) == lax.broadcasted_iota(
        jnp.int32, (padded, padded), 1
    )
    for which in range(2):
        along = jnp.broadcast_to(frames[which, 0:1, 0:padded], (padded, padded))
        down = jnp.sum(jnp.where(eye, along, 0.0), axis=1, keepdims=True)
        masks[which] = jnp.where(along <= down, 1.0, 0.0)

    mine = pl.ds(pl.multiple_of(core * padded, 16), padded)
    theirs = pl.ds(pl.multiple_of((1 - core) * padded, 16), padded)

    @pl.when(section == 0)
    def _():
        fresh[...] = jnp.zeros_like(fresh)
        for part in range(2):
            fresh[part, 0:rows, 0:half_width] = x_ref[
                :, part * half_width : (part + 1) * half_width
            ]
        put = pltpu.make_async_copy(fresh, stream.at[:, mine, :], local_sem)
        put.start()
        share = remote(fresh, stream.at[:, mine, :], pair_send.at[2], pair_recv.at[2], pair, section)
        share.start()
        put.wait()
        share.wait()

    for step in range(1, z_count):
        pass_on(0, step)
        pass_on(1, step)
    pass_on(2, 0)
    last_arrivals(0)
    last_arrivals(1)

    @pl.when(section == 1)
    def _():
        for step in range(1, z_count):
            pass_on(2, step)
        arrive = remote(
            stream.at[core], stream.at[core], y_send, y_recv, span, 1 - section
        )
        arrive.wait_recv()
        share = remote(
            stream.at[core], stream.at[core], pair_send.at[2], pair_recv.at[2], pair, section
        )
        share.start()
        share.wait()

    wide = [stream[part].astype(f32) for part in range(2)]
    square = sum(jnp.sum(value * value, axis=1, keepdims=True) for value in wide)
    inverse = lax.rsqrt(square / width + EPS)
    for part in range(2):
        scaled = (wide[part] * inverse * norm_scale[part : part + 1, :]).astype(bf16)
        normed[part] = jnp.dot(scaled, to_blocks[...], preferred_element_type=f32).astype(bf16)
    lanes = heads * LANES
    half_chips = chips // 2

    def weight_of(ref, part):
        block = ref[part * half_chips : (part + 1) * half_chips]
        return block.reshape(half_chips * block_rows, ref.shape[2])

    for index, ref in enumerate((held_a, held_b)):
        projected[:, index * cut_at : (index + 1) * cut_at] = (
            jnp.dot(normed[0], weight_of(ref, 0), preferred_element_type=f32)
            + jnp.dot(normed[1], weight_of(ref, 1), preferred_element_type=f32)
        ).astype(bf16)
    for third, into in ((1, keys), (2, values), (0, queries)):
        result = jnp.dot(
            projected[:, window_at[third] : window_at[third] + window], to_heads[third],
            preferred_element_type=f32,
        )
        into[...] = (result if third == 2 else jnp.maximum(result, 0.0)).astype(bf16)

    def pass_out(step):
        @pl.when(section == 0)
        def _():
            pass_on(2, step)

    pass_out(1)

    contract_rows = (((0,), (0,)), ((), ()))
    for which in range(2):
        at = slice(which * padded, (which + 1) * padded)
        for head in range(heads):
            cols = slice(head * LANES, (head + 1) * LANES)
            state[which, cols, :] = lax.dot_general(
                keys[at, cols], values[at, cols], contract_rows, preferred_element_type=f32
            )
    piece = sent_state.shape[1]
    sent_state[...] = (state[0] + state[1]).astype(bf16).reshape(chips, piece, LANES)

    def exchange(source, target, sends, recvs, step):
        other = (chip + step) % chips
        return remote(
            source.at[other], target.at[chip], sends.at[other], recvs.at[chip],
            other * 2 + core, section,
        )

    def landed(target, sends, recvs, step):
        other = (chip + step) % chips
        return remote(
            target.at[other], target.at[other], sends.at[other], recvs.at[other],
            other * 2 + core, section,
        )

    for step in range(1, chips):
        exchange(sent_state, got_state, state_send, state_recv, step).start()
    got_state[pl.ds(chip, 1)] = sent_state[pl.ds(chip, 1)]

    contract_lanes = (((1,), (1,)), ((), ()))

    def local_part(which):
        at = slice(which * padded, (which + 1) * padded)
        for head in range(heads):
            cols = slice(head * LANES, (head + 1) * LANES)
            scores = lax.dot_general(
                queries[at, cols], keys[at, cols], contract_lanes, preferred_element_type=f32
            )
            scores = jnp.where(masks[which] > 0.5, scores, 0.0).astype(bf16)
            mixed[at, cols] = jnp.dot(scores, values[at, cols], preferred_element_type=f32)

    local_part(0)
    pass_out(2)
    for step in range(1, chips):
        landed(got_state, state_send, state_recv, step).wait_recv()
    running = jnp.zeros((piece, LANES), f32)
    for index in range(chips):
        sent_sum[index] = running.astype(bf16)
        running = running + got_state[index].astype(f32)
    for step in range(1, chips):
        exchange(sent_sum, got_sum, sum_send, sum_recv, step).start()
    got_sum[pl.ds(chip, 1)] = sent_sum[pl.ds(chip, 1)]
    local_part(1)
    pass_out(3)
    for step in range(1, chips):
        landed(got_sum, sum_send, sum_recv, step).wait_recv()

    carried = got_sum[...].reshape(lanes, LANES)
    for which in range(2):
        at = slice(which * padded, (which + 1) * padded)
        for head in range(heads):
            cols = slice(head * LANES, (head + 1) * LANES)
            earlier = carried[cols, :]
            if which == 1:
                earlier = (earlier.astype(f32) + state[0, cols, :]).astype(bf16)
            mixture = mixed[at, cols] + jnp.dot(
                queries[at, cols], earlier, preferred_element_type=f32
            )
            size = jnp.sum(mixture * mixture, axis=1, keepdims=True) / HEAD
            queries[at, cols] = (
                mixture * lax.rsqrt(size + EPS) * head_scale[pl.ds(core * heads + head, 1), :]
            ).astype(bf16)
    fresh_heads = jnp.dot(queries[...], from_heads[...], preferred_element_type=f32)
    attended[pl.ds(core, 1)] = fresh_heads.astype(bf16)[None]
    swap = remote(attended.at[core], attended.at[core], pair_send.at[3], pair_recv.at[3], pair, section)
    swap.start()
    swap.wait()

    last_arrivals(2)
    total = stream[pl.ds(core, 1)].astype(f32)[0]
    for part in range(2):
        total = total + jnp.dot(attended[part], weight_of(held_out, part), preferred_element_type=f32)
    mixed_out = total.astype(bf16)
    keys[...] = mixed_out

    @pl.when(section == 0)
    def _():
        remote(keys, stream.at[core], y_send, y_recv, span, 1 - section).start()

    back = remote(keys.at[theirs, :], y_ref.at[core], pair_send.at[4], pair_recv.at[4], pair, section)
    back.start()
    keep = pltpu.make_async_copy(keys.at[mine, :], y_ref.at[core], local_sem)
    keep.start()
    keep.wait()
    back.wait()

    @pl.when(section == 0)
    def _():
        remote(keys, stream.at[core], y_send, y_recv, span, 1 - section).wait_send()

    give.wait_send()
    for step in range(1, chips):
        exchange(sent_state, got_state, state_send, state_recv, step).wait_send()
        exchange(sent_sum, got_sum, sum_send, sum_recv, step).wait_send()
    give_out.wait_send()
    for piece in range(3):
        for z_from in range(z_count):
            block = z_from * 2 + x_at
            forward(piece, 2, block, x_near).wait_send()

            @pl.when((z_from <= z_at) & (z_at < z_count - 1))
            def _():
                forward(piece, 0, block, span + 4).wait_send()

            @pl.when((z_from >= z_at) & (z_at > 0))
            def _():
                forward(piece, 1, block, span - 4).wait_send()


def fused(clip_tokens, frame_ids, norm_gain, qkv_weight, head_gain, out_weight):
    shards = lax.axis_size("span")
    rows, width = clip_tokens.shape
    half_width = width // 2
    kept = width // shards
    heads = half_width // HEAD
    shard_rows = whole_tiles(kept, 16)
    padded = whole_tiles(rows, 16)
    half_lanes = whole_tiles(half_width, LANES)
    lanes = heads * LANES
    chips = shards // 2
    block_rows = whole_tiles(2 * kept, 16)
    block_lanes = chips // 2 * block_rows
    cut_at = whole_tiles(3 * half_width, 2 * LANES) // 2
    window = half_lanes + LANES
    bf16, f32 = jnp.bfloat16, jnp.float32
    dma = pltpu.SemaphoreType.DMA
    vmem = pl.BlockSpec(memory_space=pltpu.VMEM)
    y = pl.pallas_call(
        layers_kernel,
        out_shape=jax.ShapeDtypeStruct((2, padded, half_lanes), bf16),
        in_specs=[vmem] * 6,
        out_specs=vmem,
        scratch_shapes=[
            pltpu.VMEM((chips, block_rows, cut_at), bf16),
            pltpu.VMEM((chips, block_rows, cut_at), bf16),
            pltpu.VMEM((chips, block_rows, half_lanes), bf16),
            pltpu.VMEM((2, shard_rows, 2 * cut_at), bf16),
            pltpu.VMEM((2, shard_rows, half_lanes), bf16),
            pltpu.VMEM((shard_rows, 2 * cut_at), bf16),
            pltpu.VMEM((shard_rows, half_lanes), bf16),
            pltpu.VMEM((2, 2 * padded, half_lanes), bf16),
            pltpu.VMEM((2, 2 * padded, block_lanes), bf16),
            pltpu.VMEM((2 * padded, 2 * cut_at), bf16),
            pltpu.VMEM((2 * padded, lanes), bf16),
            pltpu.VMEM((2 * padded, lanes), bf16),
            pltpu.VMEM((2 * padded, lanes), bf16),
            pltpu.VMEM((2 * padded, lanes), f32),
            pltpu.VMEM((2, 2 * padded, block_lanes), bf16),
            pltpu.VMEM((2, padded, half_lanes), bf16),
            pltpu.VMEM((2, lanes, LANES), f32),
            pltpu.VMEM((chips, lanes // chips, LANES), bf16),
            pltpu.VMEM((chips, lanes // chips, LANES), bf16),
            pltpu.VMEM((chips, lanes // chips, LANES), bf16),
            pltpu.VMEM((chips, lanes // chips, LANES), bf16),
            pltpu.VMEM((2, 8, whole_tiles(padded, LANES)), f32),
            pltpu.VMEM((2, padded, padded), f32),
            pltpu.VMEM((8, half_lanes), f32),
            pltpu.VMEM((whole_tiles(2 * heads, 8), LANES), f32),
            pltpu.VMEM((half_lanes, block_lanes), bf16),
            pltpu.VMEM((lanes, block_lanes), bf16),
            pltpu.VMEM((3, window, lanes), bf16),
            dma((9, chips)),
            dma((3, chips)),
            dma((6,)),
            dma((6,)),
            dma((chips,)),
            dma((chips,)),
            dma((chips,)),
            dma((chips,)),
            dma,
            dma,
            dma,
        ],
        compiler_params=pltpu.CompilerParams(
            collective_id=0, has_side_effects=True, vmem_limit_bytes=48 * 1024 * 1024
        ),
    )(
        clip_tokens,
        frame_ids.reshape(1, rows),
        norm_gain,
        qkv_weight.reshape(kept, -1),
        head_gain,
        out_weight.reshape(kept, width),
    )
    halves = y[:, :rows, :half_width]
    return jnp.concatenate([halves[0], halves[1]], axis=1)[None]


def grid_fits(mesh):
    return mesh.shape["span"] == 16 and mesh.shape["section"] == 2


def solution(mesh):
    return jax.shard_map(
        fused if grid_fits(mesh) else on_device,
        mesh=mesh,
        in_specs=(
            P("span", None),
            P("span"),
            P("section", None),
            P("section", "span"),
            P("section", None),
            P("section", "span"),
        ),
        out_specs=P("section", "span", None),
        check_vma=False,
    )
```

```python
import jax
import jax.numpy as jnp
from jax import lax
from jax.experimental import pallas as pl
from jax.experimental.pallas import tpu as pltpu
from jax.sharding import PartitionSpec as P

HEAD = 112
LANES = 128
EPS = 1e-06


def shifted(block, axis, distance):
    devices = range(lax.axis_size(axis))
    route = [(i - distance, i) for i in devices if i - distance in devices]
    return lax.ppermute(block, axis, route)


def on_device(clip_tokens, frame_ids, norm_gain, qkv_weight, head_gain, out_weight):
    row_count = clip_tokens.shape[0]
    model_width = clip_tokens.shape[1]
    qkv_flat, out_flat = (
        lax.all_gather(qkv_weight, "span", axis=1, tiled=True),
        lax.all_gather(out_weight, "span", axis=1, tiled=True),
    )
    w_qkv = qkv_flat.reshape(model_width, -1)
    inner_width = w_qkv.shape[1] // 3
    w_out = out_flat.reshape(inner_width, model_width)
    head_count = inner_width // HEAD
    norm_scale = norm_gain[0]
    head_scale = head_gain[0].reshape(head_count, HEAD)
    allowed = frame_ids[None, :] <= frame_ids[:, None]
    section_count = lax.axis_size("section")
    span_count = lax.axis_size("span")
    my_section = lax.axis_index("section")

    def project(current):
        current_wide = current.astype(jnp.float32)
        normed = (
            current_wide
            * lax.rsqrt(jnp.mean(current_wide * current_wide, axis=1, keepdims=True) + 1e-06)
            * norm_scale
        ).astype(jnp.bfloat16)
        projected = jnp.dot(normed, w_qkv, preferred_element_type=jnp.float32)
        queries = (
            jnp.maximum(projected[:, :inner_width], 0.0)
            .astype(jnp.bfloat16)
            .reshape(row_count, head_count, HEAD)
        )
        key_feats = (
            jnp.maximum(projected[:, inner_width : 2 * inner_width], 0.0)
            .astype(jnp.bfloat16)
            .reshape(row_count, head_count, HEAD)
        )
        value_rows = (
            projected[:, 2 * inner_width :]
            .astype(jnp.bfloat16)
            .reshape(row_count, head_count, HEAD)
        )
        span_state = jnp.einsum(
            "jhd,jhe->hde", key_feats, value_rows, preferred_element_type=jnp.float32
        )
        return (queries, key_feats, value_rows, span_state)

    def local_term(queries, key_feats, value_rows):
        scores = jnp.einsum("ihd,jhd->hij", queries, key_feats, preferred_element_type=jnp.float32)
        weights = jnp.where(allowed[None, :, :], scores, 0.0).astype(jnp.bfloat16)
        return jnp.einsum("hij,jhd->ihd", weights, value_rows, preferred_element_type=jnp.float32)

    def finish(current, queries, local_part, carried):
        mixture = local_part + jnp.einsum(
            "ihd,hde->ihe", queries, carried, preferred_element_type=jnp.float32
        )
        attended = (
            mixture
            * lax.rsqrt(jnp.mean(mixture * mixture, axis=2, keepdims=True) + 1e-06)
            * head_scale
        ).astype(jnp.bfloat16)
        attended = attended.reshape(row_count, inner_width)
        return (
            current.astype(jnp.float32)
            + jnp.dot(attended, w_out, preferred_element_type=jnp.float32)
        ).astype(jnp.bfloat16)

    def prefix(span_state):
        sliced = span_state.reshape(span_count, -1)
        owned = lax.all_to_all(sliced, "span", split_axis=0, concat_axis=0, tiled=True)
        running = jnp.cumsum(owned, axis=0)
        earlier = (running - owned).astype(jnp.bfloat16)
        returned = lax.all_to_all(earlier, "span", split_axis=0, concat_axis=0, tiled=True)
        return returned.reshape(span_state.shape)

    empty_heads = jnp.zeros((row_count, head_count, HEAD), jnp.bfloat16)
    empty_state = jnp.zeros((head_count, HEAD, HEAD), jnp.float32)

    def step(step_index, loop_state):
        current, result = loop_state
        active = my_section == step_index

        def early_on(operand):
            return project(operand)

        def early_off(operand):
            return (empty_heads, empty_heads, empty_heads, empty_state)

        queries, key_feats, value_rows, span_state = lax.cond(active, early_on, early_off, current)
        carried = prefix(span_state)

        def late_on(operands):
            local_part = local_term(operands[1], operands[2], operands[3])
            return finish(operands[0], operands[1], local_part, operands[4])

        def late_off(operands):
            return jnp.zeros_like(operands[0])

        updated = lax.cond(
            active, late_on, late_off, (current, queries, key_feats, value_rows, carried)
        )
        result = jnp.where(active, updated, result)
        arrived = shifted(updated, "section", 1)
        return (arrived, result)

    initial = (clip_tokens, jnp.zeros_like(clip_tokens))
    final_state = lax.fori_loop(0, section_count, step, initial)
    return final_state[1][None, :, :]


def whole_tiles(count, tile):
    return -(-count // tile) * tile


def remote(src, dst, send, recv, span, section):
    return pltpu.make_async_remote_copy(
        src_ref=src,
        dst_ref=dst,
        send_sem=send,
        recv_sem=recv,
        device_id={"span": span, "section": section},
        device_id_type=pl.DeviceIdType.MESH,
    )


def spread(size_in, size_out, group_in, kept_in, group_out, kept_out, skipped=0):
    row = lax.broadcasted_iota(jnp.int32, (size_in, size_out), 0) + (group_in - skipped)
    col = lax.broadcasted_iota(jnp.int32, (size_in, size_out), 1)
    row_in, col_in = row % group_in, col % group_out
    row_feature = (row // group_in - 1) * kept_in + row_in
    col_feature = col // group_out * kept_out + col_in
    same = (row_feature == col_feature) & (row_in < kept_in) & (col_in < kept_out)
    return jnp.where(same, 1.0, 0.0).astype(jnp.bfloat16)


def layers_kernel(
    x_ref, frame_ref, norm_ref, qkv_ref, head_ref, out_w_ref, y_ref,
    held_a, held_b, held_out, relay, packed, packed_out, got, got_out, stream, normed, projected, queries, keys, values, mixed, attended, fresh,
    state, sent_state, got_state, sent_sum, got_sum,
    frames, masks, norm_scale, head_scale, to_blocks, from_heads, to_heads,
    gather_send, gather_recv, hop_send, hop_recv, pair_send, pair_recv, state_send, state_recv,
    sum_send, sum_recv, y_send, y_recv, local_sem,
):
    f32, bf16 = jnp.float32, jnp.bfloat16
    span = lax.axis_index("span")
    section = lax.axis_index("section")
    core = span % 2
    chip = span // 2
    x_at = chip % 2
    z_at = chip // 2
    pair = span + 1 - 2 * core
    x_near = span + 2 - 4 * x_at
    chips = got_state.shape[0]
    z_count = chips // 2
    block_rows = held_a.shape[1]
    cut_at, window = held_a.shape[2], to_heads.shape[1]
    rows = x_ref.shape[0]
    padded = stream.shape[1] // 2
    half_width = x_ref.shape[1] // 2
    half_lanes = stream.shape[2]
    heads = half_width // HEAD
    kept = qkv_ref.shape[0]
    width = 2 * half_width

    frames[...] = jnp.zeros_like(frames)
    frames[pl.ds(core, 1), 0:1, 0:rows] = frame_ref[...].astype(f32)[None]

    barrier = pltpu.get_barrier_semaphore()
    for step in range(1, chips):
        other = (chip + step) % chips * 2 + core
        pl.semaphore_signal(
            barrier, inc=1, device_id={"span": other, "section": section},
            device_id_type=pl.DeviceIdType.MESH,
        )
    pl.semaphore_signal(
        barrier, inc=1, device_id={"span": pair, "section": section},
        device_id_type=pl.DeviceIdType.MESH,
    )
    pl.semaphore_signal(
        barrier, inc=1, device_id={"span": span, "section": 1 - section},
        device_id_type=pl.DeviceIdType.MESH,
    )

    packed[...] = jnp.zeros_like(packed)
    packed_out[...] = jnp.zeros_like(packed_out)
    for part in range(2):
        for third in range(3):
            at = third * width + part * half_width
            to = third * half_width
            packed[part, 0:kept, to : to + half_width] = qkv_ref[:, at : at + half_width]
        packed_out[part, 0:kept, 0:half_width] = out_w_ref[
            :, part * half_width : (part + 1) * half_width
        ]

    pl.semaphore_wait(barrier, chips + 1)

    give = remote(packed.at[1 - core], got, pair_send.at[0], pair_recv.at[0], pair, section)
    give.start()
    give_out = remote(packed_out.at[1 - core], got_out, pair_send.at[5], pair_recv.at[5], pair, section)
    give_out.start()
    give_frames = remote(frames.at[core], frames.at[core], pair_send.at[1], pair_recv.at[1], pair, section)
    give_frames.start()

    here = pl.ds(chip, 1)
    pieces = (held_a, held_b, held_out, relay)
    for piece_ref in pieces[:3]:
        piece_ref[here, 2 * kept : block_rows, :] = jnp.zeros(
            (1, block_rows - 2 * kept, piece_ref.shape[2]), bf16
        )
    give.wait_recv()
    for which in range(2):

        @pl.when(core == which)
        def _():
            a, b = slice(which * kept, (which + 1) * kept), slice((1 - which) * kept, (2 - which) * kept)
            held_a[here, a, :] = packed[which, 0:kept, 0:cut_at][None]
            held_a[here, b, :] = got[0:kept, 0:cut_at][None]
            held_b[here, a, :] = packed[which, 0:kept, cut_at:][None]
            held_b[here, b, :] = got[0:kept, cut_at:][None]

    def forward(piece, lane, block, target):
        return remote(
            pieces[piece].at[block], pieces[piece].at[block],
            gather_send.at[piece * 3 + lane, block], gather_recv.at[piece, block],
            target, section,
        )

    def pass_on(piece, step):
        if step == 0:

            @pl.when(z_at < z_count - 1)
            def _():
                forward(piece, 0, chip, span + 4).start()

            @pl.when(z_at > 0)
            def _():
                forward(piece, 1, chip, span - 4).start()

            forward(piece, 2, chip, x_near).start()
        else:
            below = (z_at - step) * 2 + x_at
            above = (z_at + step) * 2 + x_at

            @pl.when(z_at >= step)
            def _():
                forward(piece, 2, below, x_near).wait_recv()

                @pl.when(z_at < z_count - 1)
                def _():
                    forward(piece, 0, below, span + 4).start()

                forward(piece, 2, below, x_near).start()

            @pl.when(z_at + step < z_count)
            def _():
                forward(piece, 2, above, x_near).wait_recv()

                @pl.when(z_at > 0)
                def _():
                    forward(piece, 1, above, span - 4).start()

                forward(piece, 2, above, x_near).start()

    def last_arrivals(piece):
        for z_from in range(z_count):
            forward(piece, 2, z_from * 2 + (1 - x_at), x_near).wait_recv()

    def hop(source, target, block):
        return remote(
            source.at[block], target.at[block], hop_send.at[block], hop_recv.at[block],
            span, 1 - section,
        )

    def hop_back(step):
        if step > 0:

            @pl.when(z_at >= step)
            def _():
                hop(relay, held_b, (z_at - step) * 2 + x_at).start()

            @pl.when(z_at + step < z_count)
            def _():
                hop(relay, held_b, (z_at + step) * 2 + x_at).start()

        near = 1 - x_at

        @pl.when(z_at >= step)
        def _():
            block = (z_at - step) * 2 + near
            forward(3, 2, block, x_near).wait_recv()
            hop(relay, held_b, block).start()

        if step > 0:

            @pl.when(z_at + step < z_count)
            def _():
                block = (z_at + step) * 2 + near
                forward(3, 2, block, x_near).wait_recv()
                hop(relay, held_b, block).start()

    @pl.when(section == 0)
    def _():
        hop(held_b, relay, chip).start()
        pass_on(0, 0)

    @pl.when(section == 1)
    def _():
        hop(held_b, relay, chip).wait_recv()
        pass_on(3, 0)
        pass_on(0, 0)

    give_out.wait_recv()
    for which in range(2):

        @pl.when(core == which)
        def _():
            a, b = slice(which * kept, (which + 1) * kept), slice((1 - which) * kept, (2 - which) * kept)
            held_out[here, a, :] = packed_out[which, 0:kept, :][None]
            held_out[here, b, :] = got_out[0:kept, :][None]

    block_lanes = normed.shape[2]
    to_blocks[...] = spread(half_lanes, block_lanes, half_lanes, half_width, block_rows, 2 * kept)
    from_heads[...] = spread(heads * LANES, block_lanes, LANES, HEAD, block_rows, 2 * kept)
    window_at = [third * half_width // LANES * LANES for third in range(3)]
    for third in range(3):
        to_heads[third] = spread(
            window, heads * LANES, window, half_width, LANES, HEAD, third * half_width - window_at[third]
        )
    norm_scale[...] = jnp.zeros_like(norm_scale)
    for part in range(2):
        norm_scale[part : part + 1, 0:half_width] = norm_ref[
            :, part * half_width : (part + 1) * half_width
        ]
    head_scale[...] = jnp.zeros_like(head_scale)
    for head in range(2 * heads):
        head_scale[head : head + 1, 0:HEAD] = head_ref[:, head * HEAD : (head + 1) * HEAD]
    give_frames.wait()
    eye = lax.broadcasted_iota(jnp.int32, (padded, padded), 0) == lax.broadcasted_iota(
        jnp.int32, (padded, padded), 1
    )
    for which in range(2):
        along = jnp.broadcast_to(frames[which, 0:1, 0:padded], (padded, padded))
        down = jnp.sum(jnp.where(eye, along, 0.0), axis=1, keepdims=True)
        masks[which] = jnp.where(along <= down, 1.0, 0.0)

    mine = pl.ds(pl.multiple_of(core * padded, 16), padded)
    theirs = pl.ds(pl.multiple_of((1 - core) * padded, 16), padded)

    @pl.when(section == 0)
    def _():
        fresh[...] = jnp.zeros_like(fresh)
        for part in range(2):
            fresh[part, 0:rows, 0:half_width] = x_ref[
                :, part * half_width : (part + 1) * half_width
            ]
        put = pltpu.make_async_copy(fresh, stream.at[:, mine, :], local_sem)
        put.start()
        share = remote(fresh, stream.at[:, mine, :], pair_send.at[2], pair_recv.at[2], pair, section)
        share.start()
        put.wait()
        share.wait()

    @pl.when(section == 0)
    def _():
        for step in range(1, z_count):
            pass_on(0, step)
        pass_on(2, 0)
        last_arrivals(0)
        for step in range(1, chips):
            hop(relay, held_b, (chip + step) % chips).wait_recv()

    @pl.when(section == 1)
    def _():
        for step in range(1, z_count):
            pass_on(3, step)
            hop_back(step - 1)
        pass_on(1, 0)
        hop_back(z_count - 1)
        for step in range(1, z_count):
            pass_on(0, step)
            pass_on(1, step)
        pass_on(2, 0)
        last_arrivals(0)
        last_arrivals(1)

    @pl.when(section == 1)
    def _():
        for step in range(1, z_count):
            pass_on(2, step)
        arrive = remote(
            stream.at[core], stream.at[core], y_send, y_recv, span, 1 - section
        )
        arrive.wait_recv()
        share = remote(
            stream.at[core], stream.at[core], pair_send.at[2], pair_recv.at[2], pair, section
        )
        share.start()
        share.wait()

    wide = [stream[part].astype(f32) for part in range(2)]
    square = sum(jnp.sum(value * value, axis=1, keepdims=True) for value in wide)
    inverse = lax.rsqrt(square / width + EPS)
    for part in range(2):
        scaled = (wide[part] * inverse * norm_scale[part : part + 1, :]).astype(bf16)
        normed[part] = jnp.dot(scaled, to_blocks[...], preferred_element_type=f32).astype(bf16)
    lanes = heads * LANES
    half_chips = chips // 2

    def weight_of(ref, part):
        block = ref[part * half_chips : (part + 1) * half_chips]
        return block.reshape(half_chips * block_rows, ref.shape[2])

    for ref, lo, hi in ((held_a, 0, cut_at), (held_b, cut_at, projected.shape[1])):
        projected[:, lo:hi] = (
            jnp.dot(normed[0], weight_of(ref, 0), preferred_element_type=f32)
            + jnp.dot(normed[1], weight_of(ref, 1), preferred_element_type=f32)
        ).astype(bf16)
    for third, into in ((1, keys), (2, values), (0, queries)):
        result = jnp.dot(
            projected[:, window_at[third] : window_at[third] + window], to_heads[third],
            preferred_element_type=f32,
        )
        into[...] = (result if third == 2 else jnp.maximum(result, 0.0)).astype(bf16)

    def pass_out(step):
        @pl.when(section == 0)
        def _():
            pass_on(2, step)

    pass_out(1)

    contract_rows = (((0,), (0,)), ((), ()))
    for which in range(2):
        at = slice(which * padded, (which + 1) * padded)
        for head in range(heads):
            cols = slice(head * LANES, (head + 1) * LANES)
            state[which, cols, :] = lax.dot_general(
                keys[at, cols], values[at, cols], contract_rows, preferred_element_type=f32
            )
    piece = sent_state.shape[1]
    sent_state[...] = (state[0] + state[1]).astype(bf16).reshape(chips, piece, LANES)

    def exchange(source, target, sends, recvs, step):
        other = (chip + step) % chips
        return remote(
            source.at[other], target.at[chip], sends.at[other], recvs.at[chip],
            other * 2 + core, section,
        )

    def landed(target, sends, recvs, step):
        other = (chip + step) % chips
        return remote(
            target.at[other], target.at[other], sends.at[other], recvs.at[other],
            other * 2 + core, section,
        )

    for step in range(1, chips):
        exchange(sent_state, got_state, state_send, state_recv, step).start()
    got_state[pl.ds(chip, 1)] = sent_state[pl.ds(chip, 1)]

    contract_lanes = (((1,), (1,)), ((), ()))

    def local_part(which):
        at = slice(which * padded, (which + 1) * padded)
        for head in range(heads):
            cols = slice(head * LANES, (head + 1) * LANES)
            scores = lax.dot_general(
                queries[at, cols], keys[at, cols], contract_lanes, preferred_element_type=f32
            )
            scores = jnp.where(masks[which] > 0.5, scores, 0.0).astype(bf16)
            mixed[at, cols] = jnp.dot(scores, values[at, cols], preferred_element_type=f32)

    local_part(0)
    pass_out(2)
    for step in range(1, chips):
        landed(got_state, state_send, state_recv, step).wait_recv()
    running = jnp.zeros((piece, LANES), f32)
    for index in range(chips):
        sent_sum[index] = running.astype(bf16)
        running = running + got_state[index].astype(f32)
    for step in range(1, chips):
        exchange(sent_sum, got_sum, sum_send, sum_recv, step).start()
    got_sum[pl.ds(chip, 1)] = sent_sum[pl.ds(chip, 1)]
    local_part(1)
    pass_out(3)
    for step in range(1, chips):
        landed(got_sum, sum_send, sum_recv, step).wait_recv()

    carried = got_sum[...].reshape(lanes, LANES)
    for which in range(2):
        at = slice(which * padded, (which + 1) * padded)
        for head in range(heads):
            cols = slice(head * LANES, (head + 1) * LANES)
            earlier = carried[cols, :]
            if which == 1:
                earlier = (earlier.astype(f32) + state[0, cols, :]).astype(bf16)
            mixture = mixed[at, cols] + jnp.dot(
                queries[at, cols], earlier, preferred_element_type=f32
            )
            size = jnp.sum(mixture * mixture, axis=1, keepdims=True) / HEAD
            queries[at, cols] = (
                mixture * lax.rsqrt(size + EPS) * head_scale[pl.ds(core * heads + head, 1), :]
            ).astype(bf16)
    fresh_heads = jnp.dot(queries[...], from_heads[...], preferred_element_type=f32)
    attended[pl.ds(core, 1)] = fresh_heads.astype(bf16)[None]
    swap = remote(attended.at[core], attended.at[core], pair_send.at[3], pair_recv.at[3], pair, section)
    swap.start()
    swap.wait()

    last_arrivals(2)
    total = stream[pl.ds(core, 1)].astype(f32)[0]
    for part in range(2):
        total = total + jnp.dot(attended[part], weight_of(held_out, part), preferred_element_type=f32)
    mixed_out = total.astype(bf16)
    keys[...] = mixed_out

    @pl.when(section == 0)
    def _():
        remote(keys, stream.at[core], y_send, y_recv, span, 1 - section).start()

    back = remote(keys.at[theirs, :], y_ref.at[core], pair_send.at[4], pair_recv.at[4], pair, section)
    back.start()
    keep = pltpu.make_async_copy(keys.at[mine, :], y_ref.at[core], local_sem)
    keep.start()
    keep.wait()
    back.wait()

    @pl.when(section == 0)
    def _():
        remote(keys, stream.at[core], y_send, y_recv, span, 1 - section).wait_send()

    give.wait_send()
    for step in range(1, chips):
        exchange(sent_state, got_state, state_send, state_recv, step).wait_send()
        exchange(sent_sum, got_sum, sum_send, sum_recv, step).wait_send()
    give_out.wait_send()
    def sends_end(piece):
        for z_from in range(z_count):
            block = z_from * 2 + x_at
            forward(piece, 2, block, x_near).wait_send()

            @pl.when((z_from <= z_at) & (z_at < z_count - 1))
            def _():
                forward(piece, 0, block, span + 4).wait_send()

            @pl.when((z_from >= z_at) & (z_at > 0))
            def _():
                forward(piece, 1, block, span - 4).wait_send()

    sends_end(0)
    sends_end(2)

    @pl.when(section == 0)
    def _():
        hop(held_b, relay, chip).wait_send()

    @pl.when(section == 1)
    def _():
        sends_end(1)
        sends_end(3)
        for step in range(1, chips):
            hop(relay, held_b, (chip + step) % chips).wait_send()


def fused(clip_tokens, frame_ids, norm_gain, qkv_weight, head_gain, out_weight):
    shards = lax.axis_size("span")
    rows, width = clip_tokens.shape
    half_width = width // 2
    kept = width // shards
    heads = half_width // HEAD
    shard_rows = whole_tiles(kept, 16)
    padded = whole_tiles(rows, 16)
    half_lanes = whole_tiles(half_width, LANES)
    lanes = heads * LANES
    chips = shards // 2
    block_rows = whole_tiles(2 * kept, 16)
    block_lanes = chips // 2 * block_rows
    qkv_lanes = whole_tiles(3 * half_width, LANES)
    cut_at = qkv_lanes // LANES * 9 // 14 * LANES
    window = half_lanes + LANES
    bf16, f32 = jnp.bfloat16, jnp.float32
    dma = pltpu.SemaphoreType.DMA
    vmem = pl.BlockSpec(memory_space=pltpu.VMEM)
    y = pl.pallas_call(
        layers_kernel,
        out_shape=jax.ShapeDtypeStruct((2, padded, half_lanes), bf16),
        in_specs=[vmem] * 6,
        out_specs=vmem,
        scratch_shapes=[
            pltpu.VMEM((chips, block_rows, cut_at), bf16),
            pltpu.VMEM((chips, block_rows, qkv_lanes - cut_at), bf16),
            pltpu.VMEM((chips, block_rows, half_lanes), bf16),
            pltpu.VMEM((chips, block_rows, qkv_lanes - cut_at), bf16),
            pltpu.VMEM((2, shard_rows, qkv_lanes), bf16),
            pltpu.VMEM((2, shard_rows, half_lanes), bf16),
            pltpu.VMEM((shard_rows, qkv_lanes), bf16),
            pltpu.VMEM((shard_rows, half_lanes), bf16),
            pltpu.VMEM((2, 2 * padded, half_lanes), bf16),
            pltpu.VMEM((2, 2 * padded, block_lanes), bf16),
            pltpu.VMEM((2 * padded, qkv_lanes), bf16),
            pltpu.VMEM((2 * padded, lanes), bf16),
            pltpu.VMEM((2 * padded, lanes), bf16),
            pltpu.VMEM((2 * padded, lanes), bf16),
            pltpu.VMEM((2 * padded, lanes), f32),
            pltpu.VMEM((2, 2 * padded, block_lanes), bf16),
            pltpu.VMEM((2, padded, half_lanes), bf16),
            pltpu.VMEM((2, lanes, LANES), f32),
            pltpu.VMEM((chips, lanes // chips, LANES), bf16),
            pltpu.VMEM((chips, lanes // chips, LANES), bf16),
            pltpu.VMEM((chips, lanes // chips, LANES), bf16),
            pltpu.VMEM((chips, lanes // chips, LANES), bf16),
            pltpu.VMEM((2, 8, whole_tiles(padded, LANES)), f32),
            pltpu.VMEM((2, padded, padded), f32),
            pltpu.VMEM((8, half_lanes), f32),
            pltpu.VMEM((whole_tiles(2 * heads, 8), LANES), f32),
            pltpu.VMEM((half_lanes, block_lanes), bf16),
            pltpu.VMEM((lanes, block_lanes), bf16),
            pltpu.VMEM((3, window, lanes), bf16),
            dma((12, chips)),
            dma((4, chips)),
            dma((chips,)),
            dma((chips,)),
            dma((6,)),
            dma((6,)),
            dma((chips,)),
            dma((chips,)),
            dma((chips,)),
            dma((chips,)),
            dma,
            dma,
            dma,
        ],
        compiler_params=pltpu.CompilerParams(
            collective_id=0, has_side_effects=True, vmem_limit_bytes=48 * 1024 * 1024
        ),
    )(
        clip_tokens,
        frame_ids.reshape(1, rows),
        norm_gain,
        qkv_weight.reshape(kept, -1),
        head_gain,
        out_weight.reshape(kept, width),
    )
    halves = y[:, :rows, :half_width]
    return jnp.concatenate([halves[0], halves[1]], axis=1)[None]


def grid_fits(mesh):
    return mesh.shape["span"] == 16 and mesh.shape["section"] == 2


def solution(mesh):
    return jax.shard_map(
        fused if grid_fits(mesh) else on_device,
        mesh=mesh,
        in_specs=(
            P("span", None),
            P("span"),
            P("section", None),
            P("section", "span"),
            P("section", None),
            P("section", "span"),
        ),
        out_specs=P("section", "span", None),
        check_vma=False,
    )
```

```python
import jax
import jax.numpy as jnp
from jax import lax
from jax.experimental import pallas as pl
from jax.experimental.pallas import tpu as pltpu
from jax.sharding import PartitionSpec as P

HEAD = 112
LANES = 128
EPS = 1e-06


def shifted(block, axis, distance):
    devices = range(lax.axis_size(axis))
    route = [(i - distance, i) for i in devices if i - distance in devices]
    return lax.ppermute(block, axis, route)


def on_device(clip_tokens, frame_ids, norm_gain, qkv_weight, head_gain, out_weight):
    row_count = clip_tokens.shape[0]
    model_width = clip_tokens.shape[1]
    qkv_flat, out_flat = (
        lax.all_gather(qkv_weight, "span", axis=1, tiled=True),
        lax.all_gather(out_weight, "span", axis=1, tiled=True),
    )
    w_qkv = qkv_flat.reshape(model_width, -1)
    inner_width = w_qkv.shape[1] // 3
    w_out = out_flat.reshape(inner_width, model_width)
    head_count = inner_width // HEAD
    norm_scale = norm_gain[0]
    head_scale = head_gain[0].reshape(head_count, HEAD)
    allowed = frame_ids[None, :] <= frame_ids[:, None]
    section_count = lax.axis_size("section")
    span_count = lax.axis_size("span")
    my_section = lax.axis_index("section")

    def project(current):
        current_wide = current.astype(jnp.float32)
        normed = (
            current_wide
            * lax.rsqrt(jnp.mean(current_wide * current_wide, axis=1, keepdims=True) + 1e-06)
            * norm_scale
        ).astype(jnp.bfloat16)
        projected = jnp.dot(normed, w_qkv, preferred_element_type=jnp.float32)
        queries = (
            jnp.maximum(projected[:, :inner_width], 0.0)
            .astype(jnp.bfloat16)
            .reshape(row_count, head_count, HEAD)
        )
        key_feats = (
            jnp.maximum(projected[:, inner_width : 2 * inner_width], 0.0)
            .astype(jnp.bfloat16)
            .reshape(row_count, head_count, HEAD)
        )
        value_rows = (
            projected[:, 2 * inner_width :]
            .astype(jnp.bfloat16)
            .reshape(row_count, head_count, HEAD)
        )
        span_state = jnp.einsum(
            "jhd,jhe->hde", key_feats, value_rows, preferred_element_type=jnp.float32
        )
        return (queries, key_feats, value_rows, span_state)

    def local_term(queries, key_feats, value_rows):
        scores = jnp.einsum("ihd,jhd->hij", queries, key_feats, preferred_element_type=jnp.float32)
        weights = jnp.where(allowed[None, :, :], scores, 0.0).astype(jnp.bfloat16)
        return jnp.einsum("hij,jhd->ihd", weights, value_rows, preferred_element_type=jnp.float32)

    def finish(current, queries, local_part, carried):
        mixture = local_part + jnp.einsum(
            "ihd,hde->ihe", queries, carried, preferred_element_type=jnp.float32
        )
        attended = (
            mixture
            * lax.rsqrt(jnp.mean(mixture * mixture, axis=2, keepdims=True) + 1e-06)
            * head_scale
        ).astype(jnp.bfloat16)
        attended = attended.reshape(row_count, inner_width)
        return (
            current.astype(jnp.float32)
            + jnp.dot(attended, w_out, preferred_element_type=jnp.float32)
        ).astype(jnp.bfloat16)

    def prefix(span_state):
        sliced = span_state.reshape(span_count, -1)
        owned = lax.all_to_all(sliced, "span", split_axis=0, concat_axis=0, tiled=True)
        running = jnp.cumsum(owned, axis=0)
        earlier = (running - owned).astype(jnp.bfloat16)
        returned = lax.all_to_all(earlier, "span", split_axis=0, concat_axis=0, tiled=True)
        return returned.reshape(span_state.shape)

    empty_heads = jnp.zeros((row_count, head_count, HEAD), jnp.bfloat16)
    empty_state = jnp.zeros((head_count, HEAD, HEAD), jnp.float32)

    def step(step_index, loop_state):
        current, result = loop_state
        active = my_section == step_index

        def early_on(operand):
            return project(operand)

        def early_off(operand):
            return (empty_heads, empty_heads, empty_heads, empty_state)

        queries, key_feats, value_rows, span_state = lax.cond(active, early_on, early_off, current)
        carried = prefix(span_state)

        def late_on(operands):
            local_part = local_term(operands[1], operands[2], operands[3])
            return finish(operands[0], operands[1], local_part, operands[4])

        def late_off(operands):
            return jnp.zeros_like(operands[0])

        updated = lax.cond(
            active, late_on, late_off, (current, queries, key_feats, value_rows, carried)
        )
        result = jnp.where(active, updated, result)
        arrived = shifted(updated, "section", 1)
        return (arrived, result)

    initial = (clip_tokens, jnp.zeros_like(clip_tokens))
    final_state = lax.fori_loop(0, section_count, step, initial)
    return final_state[1][None, :, :]


def whole_tiles(count, tile):
    return -(-count // tile) * tile


def remote(src, dst, send, recv, span, section):
    return pltpu.make_async_remote_copy(
        src_ref=src,
        dst_ref=dst,
        send_sem=send,
        recv_sem=recv,
        device_id={"span": span, "section": section},
        device_id_type=pl.DeviceIdType.MESH,
    )


def spread(size_in, size_out, group_in, kept_in, group_out, kept_out, skipped=0):
    row = lax.broadcasted_iota(jnp.int32, (size_in, 1), 0) + (group_in - skipped)
    col = lax.broadcasted_iota(jnp.int32, (1, size_out), 1)
    row_in, col_in = row % group_in, col % group_out
    row_feature = jnp.where(row_in < kept_in, (row // group_in - 1) * kept_in + row_in, -1)
    col_feature = jnp.where(col_in < kept_out, col // group_out * kept_out + col_in, -2)
    same = jnp.broadcast_to(row_feature, (size_in, size_out)) == col_feature
    return jnp.where(same, 1.0, 0.0).astype(jnp.bfloat16)


def layers_kernel(
    x_ref, frame_ref, norm_ref, qkv_ref, head_ref, out_w_ref, y_ref,
    held_a, held_b, held_out, packed, packed_out, got, got_out, stream, normed, projected, queries, keys, values, mixed, attended, fresh,
    state, sent_state, got_state, sent_sum, got_sum,
    frames, masks, norm_scale, head_scale, to_blocks, from_heads, to_heads,
    gather_send, gather_recv, pair_send, pair_recv, state_send, state_recv,
    sum_send, sum_recv, y_send, y_recv, local_sem,
):
    f32, bf16 = jnp.float32, jnp.bfloat16
    span = lax.axis_index("span")
    section = lax.axis_index("section")
    core = span % 2
    chip = span // 2
    x_at = chip % 2
    z_at = chip // 2
    pair = span + 1 - 2 * core
    x_near = span + 2 - 4 * x_at
    chips = got_state.shape[0]
    z_count = chips // 2
    block_rows = held_a.shape[1]
    cut_at, window = held_a.shape[2], to_heads.shape[1]
    rows = x_ref.shape[0]
    padded = stream.shape[1] // 2
    half_width = x_ref.shape[1] // 2
    half_lanes = stream.shape[2]
    heads = half_width // HEAD
    kept = qkv_ref.shape[0]
    width = 2 * half_width

    frames[...] = jnp.zeros_like(frames)
    frames[pl.ds(core, 1), 0:1, 0:rows] = frame_ref[...].astype(f32)[None]

    barrier = pltpu.get_barrier_semaphore()
    for step in range(1, chips):
        other = (chip + step) % chips * 2 + core
        pl.semaphore_signal(
            barrier, inc=1, device_id={"span": other, "section": section},
            device_id_type=pl.DeviceIdType.MESH,
        )
    pl.semaphore_signal(
        barrier, inc=1, device_id={"span": pair, "section": section},
        device_id_type=pl.DeviceIdType.MESH,
    )
    pl.semaphore_signal(
        barrier, inc=1, device_id={"span": span, "section": 1 - section},
        device_id_type=pl.DeviceIdType.MESH,
    )

    packed[...] = jnp.zeros_like(packed)
    packed_out[...] = jnp.zeros_like(packed_out)
    for part in range(2):
        for third in range(3):
            at = third * width + part * half_width
            to = third * half_width
            packed[part, 0:kept, to : to + half_width] = qkv_ref[:, at : at + half_width]
        packed_out[part, 0:kept, 0:half_width] = out_w_ref[
            :, part * half_width : (part + 1) * half_width
        ]

    pl.semaphore_wait(barrier, chips + 1)

    give = remote(packed.at[1 - core], got, pair_send.at[0], pair_recv.at[0], pair, section)
    give.start()
    give_out = remote(packed_out.at[1 - core], got_out, pair_send.at[5], pair_recv.at[5], pair, section)
    give_out.start()
    give_frames = remote(frames.at[core], frames.at[core], pair_send.at[1], pair_recv.at[1], pair, section)
    give_frames.start()

    here = pl.ds(chip, 1)
    pieces = (held_a, held_b, held_out)
    for piece_ref in pieces:
        piece_ref[here, 2 * kept : block_rows, :] = jnp.zeros(
            (1, block_rows - 2 * kept, piece_ref.shape[2]), bf16
        )
    give.wait_recv()
    for which in range(2):

        @pl.when(core == which)
        def _():
            a, b = slice(which * kept, (which + 1) * kept), slice((1 - which) * kept, (2 - which) * kept)
            held_a[here, a, :] = packed[which, 0:kept, 0:cut_at][None]
            held_a[here, b, :] = got[0:kept, 0:cut_at][None]
            held_b[here, a, :] = packed[which, 0:kept, cut_at:][None]
            held_b[here, b, :] = got[0:kept, cut_at:][None]

    def forward(piece, lane, block, target):
        return remote(
            pieces[piece].at[block], pieces[piece].at[block],
            gather_send.at[piece * 3 + lane, block], gather_recv.at[piece, block],
            target, section,
        )

    def pass_on(piece, step):
        if step == 0:

            @pl.when(z_at < z_count - 1)
            def _():
                forward(piece, 0, chip, span + 4).start()

            @pl.when(z_at > 0)
            def _():
                forward(piece, 1, chip, span - 4).start()

            forward(piece, 2, chip, x_near).start()
        else:
            below = (z_at - step) * 2 + x_at
            above = (z_at + step) * 2 + x_at

            @pl.when(z_at >= step)
            def _():
                forward(piece, 2, below, x_near).wait_recv()

                @pl.when(z_at < z_count - 1)
                def _():
                    forward(piece, 0, below, span + 4).start()

                forward(piece, 2, below, x_near).start()

            @pl.when(z_at + step < z_count)
            def _():
                forward(piece, 2, above, x_near).wait_recv()

                @pl.when(z_at > 0)
                def _():
                    forward(piece, 1, above, span - 4).start()

                forward(piece, 2, above, x_near).start()

    def last_arrivals(piece):
        for z_from in range(z_count):
            forward(piece, 2, z_from * 2 + (1 - x_at), x_near).wait_recv()

    pass_on(0, 0)
    pass_on(1, 0)

    give_out.wait_recv()
    for which in range(2):

        @pl.when(core == which)
        def _():
            a, b = slice(which * kept, (which + 1) * kept), slice((1 - which) * kept, (2 - which) * kept)
            held_out[here, a, :] = packed_out[which, 0:kept, :][None]
            held_out[here, b, :] = got_out[0:kept, :][None]

    block_lanes = normed.shape[2]
    to_blocks[...] = spread(half_lanes, block_lanes, half_lanes, half_width, block_rows, 2 * kept)
    from_heads[...] = spread(heads * LANES, block_lanes, LANES, HEAD, block_rows, 2 * kept)
    window_at = [third * half_width // LANES * LANES for third in range(3)]
    for third in range(3):
        to_heads[third] = spread(
            window, heads * LANES, window, half_width, LANES, HEAD, third * half_width - window_at[third]
        )
    norm_scale[...] = jnp.zeros_like(norm_scale)
    for part in range(2):
        norm_scale[part : part + 1, 0:half_width] = norm_ref[
            :, part * half_width : (part + 1) * half_width
        ]
    head_scale[...] = jnp.zeros_like(head_scale)
    for head in range(2 * heads):
        head_scale[head : head + 1, 0:HEAD] = head_ref[:, head * HEAD : (head + 1) * HEAD]
    give_frames.wait()
    eye = lax.broadcasted_iota(jnp.int32, (padded, padded), 0) == lax.broadcasted_iota(
        jnp.int32, (padded, padded), 1
    )
    for which in range(2):
        along = jnp.broadcast_to(frames[which, 0:1, 0:padded], (padded, padded))
        down = jnp.sum(jnp.where(eye, along, 0.0), axis=1, keepdims=True)
        masks[which] = jnp.where(along <= down, 1.0, 0.0)

    mine = pl.ds(pl.multiple_of(core * padded, 16), padded)
    theirs = pl.ds(pl.multiple_of((1 - core) * padded, 16), padded)

    @pl.when(section == 0)
    def _():
        fresh[...] = jnp.zeros_like(fresh)
        for part in range(2):
            fresh[part, 0:rows, 0:half_width] = x_ref[
                :, part * half_width : (part + 1) * half_width
            ]
        put = pltpu.make_async_copy(fresh, stream.at[:, mine, :], local_sem)
        put.start()
        share = remote(fresh, stream.at[:, mine, :], pair_send.at[2], pair_recv.at[2], pair, section)
        share.start()
        put.wait()
        share.wait()

    for step in range(1, z_count):
        pass_on(0, step)
        pass_on(1, step)
    pass_on(2, 0)
    last_arrivals(0)
    last_arrivals(1)

    @pl.when(section == 1)
    def _():
        for step in range(1, z_count):
            pass_on(2, step)
        arrive = remote(
            stream.at[core], stream.at[core], y_send, y_recv, span, 1 - section
        )
        arrive.wait_recv()
        share = remote(
            stream.at[core], stream.at[core], pair_send.at[2], pair_recv.at[2], pair, section
        )
        share.start()
        share.wait()

    wide = [stream[part].astype(f32) for part in range(2)]
    square = sum(jnp.sum(value * value, axis=1, keepdims=True) for value in wide)
    inverse = lax.rsqrt(square / width + EPS)
    for part in range(2):
        scaled = (wide[part] * inverse * norm_scale[part : part + 1, :]).astype(bf16)
        normed[part] = jnp.dot(scaled, to_blocks[...], preferred_element_type=f32).astype(bf16)
    lanes = heads * LANES
    half_chips = chips // 2

    def weight_of(ref, part):
        block = ref[part * half_chips : (part + 1) * half_chips]
        return block.reshape(half_chips * block_rows, ref.shape[2])

    for index, ref in enumerate((held_a, held_b)):
        projected[:, index * cut_at : (index + 1) * cut_at] = (
            jnp.dot(normed[0], weight_of(ref, 0), preferred_element_type=f32)
            + jnp.dot(normed[1], weight_of(ref, 1), preferred_element_type=f32)
        ).astype(bf16)
    for third, into in ((1, keys), (2, values), (0, queries)):
        result = jnp.dot(
            projected[:, window_at[third] : window_at[third] + window], to_heads[third],
            preferred_element_type=f32,
        )
        into[...] = (result if third == 2 else jnp.maximum(result, 0.0)).astype(bf16)

    def pass_out(step):
        @pl.when(section == 0)
        def _():
            pass_on(2, step)

    pass_out(1)

    contract_rows = (((0,), (0,)), ((), ()))
    for which in range(2):
        at = slice(which * padded, (which + 1) * padded)
        for head in range(heads):
            cols = slice(head * LANES, (head + 1) * LANES)
            state[which, cols, :] = lax.dot_general(
                keys[at, cols], values[at, cols], contract_rows, preferred_element_type=f32
            )
    piece = sent_state.shape[1]
    sent_state[...] = (state[0] + state[1]).astype(bf16).reshape(chips, piece, LANES)

    def exchange(source, target, sends, recvs, step):
        other = (chip + step) % chips
        return remote(
            source.at[other], target.at[chip], sends.at[other], recvs.at[chip],
            other * 2 + core, section,
        )

    def landed(target, sends, recvs, step):
        other = (chip + step) % chips
        return remote(
            target.at[other], target.at[other], sends.at[other], recvs.at[other],
            other * 2 + core, section,
        )

    for step in range(1, chips):
        exchange(sent_state, got_state, state_send, state_recv, step).start()
    got_state[pl.ds(chip, 1)] = sent_state[pl.ds(chip, 1)]

    contract_lanes = (((1,), (1,)), ((), ()))

    def local_part(which):
        at = slice(which * padded, (which + 1) * padded)
        for head in range(heads):
            cols = slice(head * LANES, (head + 1) * LANES)
            scores = lax.dot_general(
                queries[at, cols], keys[at, cols], contract_lanes, preferred_element_type=f32
            )
            scores = jnp.where(masks[which] > 0.5, scores, 0.0).astype(bf16)
            mixed[at, cols] = jnp.dot(scores, values[at, cols], preferred_element_type=f32)

    local_part(0)
    pass_out(2)
    for step in range(1, chips):
        landed(got_state, state_send, state_recv, step).wait_recv()
    running = jnp.zeros((piece, LANES), f32)
    for index in range(chips):
        sent_sum[index] = running.astype(bf16)
        running = running + got_state[index].astype(f32)
    for step in range(1, chips):
        exchange(sent_sum, got_sum, sum_send, sum_recv, step).start()
    got_sum[pl.ds(chip, 1)] = sent_sum[pl.ds(chip, 1)]
    local_part(1)
    pass_out(3)
    for step in range(1, chips):
        landed(got_sum, sum_send, sum_recv, step).wait_recv()

    carried = got_sum[...].reshape(lanes, LANES)
    for which in range(2):
        at = slice(which * padded, (which + 1) * padded)
        for head in range(heads):
            cols = slice(head * LANES, (head + 1) * LANES)
            earlier = carried[cols, :]
            if which == 1:
                earlier = (earlier.astype(f32) + state[0, cols, :]).astype(bf16)
            mixture = mixed[at, cols] + jnp.dot(
                queries[at, cols], earlier, preferred_element_type=f32
            )
            size = jnp.sum(mixture * mixture, axis=1, keepdims=True) / HEAD
            queries[at, cols] = (
                mixture * lax.rsqrt(size + EPS) * head_scale[pl.ds(core * heads + head, 1), :]
            ).astype(bf16)
    fresh_heads = jnp.dot(queries[...], from_heads[...], preferred_element_type=f32)
    attended[pl.ds(core, 1)] = fresh_heads.astype(bf16)[None]
    swap = remote(attended.at[core], attended.at[core], pair_send.at[3], pair_recv.at[3], pair, section)
    swap.start()
    swap.wait()

    last_arrivals(2)
    total = stream[pl.ds(core, 1)].astype(f32)[0]
    for part in range(2):
        total = total + jnp.dot(attended[part], weight_of(held_out, part), preferred_element_type=f32)
    mixed_out = total.astype(bf16)
    keys[...] = mixed_out

    @pl.when(section == 0)
    def _():
        remote(keys, stream.at[core], y_send, y_recv, span, 1 - section).start()

    back = remote(keys.at[theirs, :], y_ref.at[core], pair_send.at[4], pair_recv.at[4], pair, section)
    back.start()
    keep = pltpu.make_async_copy(keys.at[mine, :], y_ref.at[core], local_sem)
    keep.start()
    keep.wait()
    back.wait()

    @pl.when(section == 0)
    def _():
        remote(keys, stream.at[core], y_send, y_recv, span, 1 - section).wait_send()

    give.wait_send()
    for step in range(1, chips):
        exchange(sent_state, got_state, state_send, state_recv, step).wait_send()
        exchange(sent_sum, got_sum, sum_send, sum_recv, step).wait_send()
    give_out.wait_send()
    for piece in range(3):
        for z_from in range(z_count):
            block = z_from * 2 + x_at
            forward(piece, 2, block, x_near).wait_send()

            @pl.when((z_from <= z_at) & (z_at < z_count - 1))
            def _():
                forward(piece, 0, block, span + 4).wait_send()

            @pl.when((z_from >= z_at) & (z_at > 0))
            def _():
                forward(piece, 1, block, span - 4).wait_send()


def fused(clip_tokens, frame_ids, norm_gain, qkv_weight, head_gain, out_weight):
    shards = lax.axis_size("span")
    rows, width = clip_tokens.shape
    half_width = width // 2
    kept = width // shards
    heads = half_width // HEAD
    shard_rows = whole_tiles(kept, 16)
    padded = whole_tiles(rows, 16)
    half_lanes = whole_tiles(half_width, LANES)
    lanes = heads * LANES
    chips = shards // 2
    block_rows = whole_tiles(2 * kept, 16)
    block_lanes = chips // 2 * block_rows
    cut_at = whole_tiles(3 * half_width, 2 * LANES) // 2
    window = half_lanes + LANES
    bf16, f32 = jnp.bfloat16, jnp.float32
    dma = pltpu.SemaphoreType.DMA
    vmem = pl.BlockSpec(memory_space=pltpu.VMEM)
    y = pl.pallas_call(
        layers_kernel,
        out_shape=jax.ShapeDtypeStruct((2, padded, half_lanes), bf16),
        in_specs=[vmem] * 6,
        out_specs=vmem,
        scratch_shapes=[
            pltpu.VMEM((chips, block_rows, cut_at), bf16),
            pltpu.VMEM((chips, block_rows, cut_at), bf16),
            pltpu.VMEM((chips, block_rows, half_lanes), bf16),
            pltpu.VMEM((2, shard_rows, 2 * cut_at), bf16),
            pltpu.VMEM((2, shard_rows, half_lanes), bf16),
            pltpu.VMEM((shard_rows, 2 * cut_at), bf16),
            pltpu.VMEM((shard_rows, half_lanes), bf16),
            pltpu.VMEM((2, 2 * padded, half_lanes), bf16),
            pltpu.VMEM((2, 2 * padded, block_lanes), bf16),
            pltpu.VMEM((2 * padded, 2 * cut_at), bf16),
            pltpu.VMEM((2 * padded, lanes), bf16),
            pltpu.VMEM((2 * padded, lanes), bf16),
            pltpu.VMEM((2 * padded, lanes), bf16),
            pltpu.VMEM((2 * padded, lanes), f32),
            pltpu.VMEM((2, 2 * padded, block_lanes), bf16),
            pltpu.VMEM((2, padded, half_lanes), bf16),
            pltpu.VMEM((2, lanes, LANES), f32),
            pltpu.VMEM((chips, lanes // chips, LANES), bf16),
            pltpu.VMEM((chips, lanes // chips, LANES), bf16),
            pltpu.VMEM((chips, lanes // chips, LANES), bf16),
            pltpu.VMEM((chips, lanes // chips, LANES), bf16),
            pltpu.VMEM((2, 8, whole_tiles(padded, LANES)), f32),
            pltpu.VMEM((2, padded, padded), f32),
            pltpu.VMEM((8, half_lanes), f32),
            pltpu.VMEM((whole_tiles(2 * heads, 8), LANES), f32),
            pltpu.VMEM((half_lanes, block_lanes), bf16),
            pltpu.VMEM((lanes, block_lanes), bf16),
            pltpu.VMEM((3, window, lanes), bf16),
            dma((9, chips)),
            dma((3, chips)),
            dma((6,)),
            dma((6,)),
            dma((chips,)),
            dma((chips,)),
            dma((chips,)),
            dma((chips,)),
            dma,
            dma,
            dma,
        ],
        compiler_params=pltpu.CompilerParams(
            collective_id=0, has_side_effects=True, vmem_limit_bytes=48 * 1024 * 1024
        ),
    )(
        clip_tokens,
        frame_ids.reshape(1, rows),
        norm_gain,
        qkv_weight.reshape(kept, -1),
        head_gain,
        out_weight.reshape(kept, width),
    )
    halves = y[:, :rows, :half_width]
    return jnp.concatenate([halves[0], halves[1]], axis=1)[None]


def grid_fits(mesh):
    return mesh.shape["span"] == 16 and mesh.shape["section"] == 2


def solution(mesh):
    return jax.shard_map(
        fused if grid_fits(mesh) else on_device,
        mesh=mesh,
        in_specs=(
            P("span", None),
            P("span"),
            P("section", None),
            P("section", "span"),
            P("section", None),
            P("section", "span"),
        ),
        out_specs=P("section", "span", None),
        check_vma=False,
    )
```

```python
import jax
import jax.numpy as jnp
from jax import lax
from jax.experimental import pallas as pl
from jax.experimental.pallas import tpu as pltpu
from jax.sharding import PartitionSpec as P

HEAD = 112
LANES = 128
EPS = 1e-06


def shifted(block, axis, distance):
    devices = range(lax.axis_size(axis))
    route = [(i - distance, i) for i in devices if i - distance in devices]
    return lax.ppermute(block, axis, route)


def on_device(clip_tokens, frame_ids, norm_gain, qkv_weight, head_gain, out_weight):
    row_count = clip_tokens.shape[0]
    model_width = clip_tokens.shape[1]
    qkv_flat, out_flat = (
        lax.all_gather(qkv_weight, "span", axis=1, tiled=True),
        lax.all_gather(out_weight, "span", axis=1, tiled=True),
    )
    w_qkv = qkv_flat.reshape(model_width, -1)
    inner_width = w_qkv.shape[1] // 3
    w_out = out_flat.reshape(inner_width, model_width)
    head_count = inner_width // HEAD
    norm_scale = norm_gain[0]
    head_scale = head_gain[0].reshape(head_count, HEAD)
    allowed = frame_ids[None, :] <= frame_ids[:, None]
    section_count = lax.axis_size("section")
    span_count = lax.axis_size("span")
    my_section = lax.axis_index("section")

    def project(current):
        current_wide = current.astype(jnp.float32)
        normed = (
            current_wide
            * lax.rsqrt(jnp.mean(current_wide * current_wide, axis=1, keepdims=True) + 1e-06)
            * norm_scale
        ).astype(jnp.bfloat16)
        projected = jnp.dot(normed, w_qkv, preferred_element_type=jnp.float32)
        queries = (
            jnp.maximum(projected[:, :inner_width], 0.0)
            .astype(jnp.bfloat16)
            .reshape(row_count, head_count, HEAD)
        )
        key_feats = (
            jnp.maximum(projected[:, inner_width : 2 * inner_width], 0.0)
            .astype(jnp.bfloat16)
            .reshape(row_count, head_count, HEAD)
        )
        value_rows = (
            projected[:, 2 * inner_width :]
            .astype(jnp.bfloat16)
            .reshape(row_count, head_count, HEAD)
        )
        span_state = jnp.einsum(
            "jhd,jhe->hde", key_feats, value_rows, preferred_element_type=jnp.float32
        )
        return (queries, key_feats, value_rows, span_state)

    def local_term(queries, key_feats, value_rows):
        scores = jnp.einsum("ihd,jhd->hij", queries, key_feats, preferred_element_type=jnp.float32)
        weights = jnp.where(allowed[None, :, :], scores, 0.0).astype(jnp.bfloat16)
        return jnp.einsum("hij,jhd->ihd", weights, value_rows, preferred_element_type=jnp.float32)

    def finish(current, queries, local_part, carried):
        mixture = local_part + jnp.einsum(
            "ihd,hde->ihe", queries, carried, preferred_element_type=jnp.float32
        )
        attended = (
            mixture
            * lax.rsqrt(jnp.mean(mixture * mixture, axis=2, keepdims=True) + 1e-06)
            * head_scale
        ).astype(jnp.bfloat16)
        attended = attended.reshape(row_count, inner_width)
        return (
            current.astype(jnp.float32)
            + jnp.dot(attended, w_out, preferred_element_type=jnp.float32)
        ).astype(jnp.bfloat16)

    def prefix(span_state):
        sliced = span_state.reshape(span_count, -1)
        owned = lax.all_to_all(sliced, "span", split_axis=0, concat_axis=0, tiled=True)
        running = jnp.cumsum(owned, axis=0)
        earlier = (running - owned).astype(jnp.bfloat16)
        returned = lax.all_to_all(earlier, "span", split_axis=0, concat_axis=0, tiled=True)
        return returned.reshape(span_state.shape)

    empty_heads = jnp.zeros((row_count, head_count, HEAD), jnp.bfloat16)
    empty_state = jnp.zeros((head_count, HEAD, HEAD), jnp.float32)

    def step(step_index, loop_state):
        current, result = loop_state
        active = my_section == step_index

        def early_on(operand):
            return project(operand)

        def early_off(operand):
            return (empty_heads, empty_heads, empty_heads, empty_state)

        queries, key_feats, value_rows, span_state = lax.cond(active, early_on, early_off, current)
        carried = prefix(span_state)

        def late_on(operands):
            local_part = local_term(operands[1], operands[2], operands[3])
            return finish(operands[0], operands[1], local_part, operands[4])

        def late_off(operands):
            return jnp.zeros_like(operands[0])

        updated = lax.cond(
            active, late_on, late_off, (current, queries, key_feats, value_rows, carried)
        )
        result = jnp.where(active, updated, result)
        arrived = shifted(updated, "section", 1)
        return (arrived, result)

    initial = (clip_tokens, jnp.zeros_like(clip_tokens))
    final_state = lax.fori_loop(0, section_count, step, initial)
    return final_state[1][None, :, :]


def whole_tiles(count, tile):
    return -(-count // tile) * tile


def remote(src, dst, send, recv, span, section):
    return pltpu.make_async_remote_copy(
        src_ref=src,
        dst_ref=dst,
        send_sem=send,
        recv_sem=recv,
        device_id={"span": span, "section": section},
        device_id_type=pl.DeviceIdType.MESH,
    )


def spread(size_in, size_out, group_in, kept_in, group_out, kept_out, skipped=0):
    row = lax.broadcasted_iota(jnp.int32, (size_in, 1), 0) + (group_in - skipped)
    col = lax.broadcasted_iota(jnp.int32, (1, size_out), 1)
    row_in, col_in = row % group_in, col % group_out
    row_feature = jnp.where(row_in < kept_in, (row // group_in - 1) * kept_in + row_in, -1)
    col_feature = jnp.where(col_in < kept_out, col // group_out * kept_out + col_in, -2)
    same = jnp.broadcast_to(row_feature, (size_in, size_out)) == col_feature
    return jnp.where(same, 1.0, 0.0).astype(jnp.bfloat16)


def layers_kernel(
    x_ref, frame_ref, norm_ref, qkv_ref, head_ref, out_w_ref, y_ref,
    held_a, held_b, held_out, packed, packed_out, got, got_out, stream, normed, projected, queries, keys, values, mixed, attended, fresh,
    state, sent_state, got_state, sent_sum, got_sum,
    frames, masks, norm_scale, head_scale, to_blocks, from_heads, to_heads,
    gather_send, gather_recv, pair_send, pair_recv, state_send, state_recv,
    sum_send, sum_recv, y_send, y_recv, local_sem,
):
    f32, bf16 = jnp.float32, jnp.bfloat16
    span = lax.axis_index("span")
    section = lax.axis_index("section")
    core = span % 2
    chip = span // 2
    x_at = chip % 2
    z_at = chip // 2
    pair = span + 1 - 2 * core
    x_near = span + 2 - 4 * x_at
    chips = got_state.shape[0]
    z_count = chips // 2
    block_rows = held_a.shape[1]
    cut_at, window = held_a.shape[2], to_heads.shape[1]
    rows = x_ref.shape[0]
    padded = stream.shape[1] // 2
    half_width = x_ref.shape[1] // 2
    half_lanes = stream.shape[2]
    heads = half_width // HEAD
    kept = qkv_ref.shape[0]
    width = 2 * half_width

    frames[...] = jnp.zeros_like(frames)
    frames[pl.ds(core, 1), 0:1, 0:rows] = frame_ref[...].astype(f32)[None]

    barrier = pltpu.get_barrier_semaphore()
    for step in range(1, chips):
        other = (chip + step) % chips * 2 + core
        pl.semaphore_signal(
            barrier, inc=1, device_id={"span": other, "section": section},
            device_id_type=pl.DeviceIdType.MESH,
        )
    pl.semaphore_signal(
        barrier, inc=1, device_id={"span": pair, "section": section},
        device_id_type=pl.DeviceIdType.MESH,
    )
    pl.semaphore_signal(
        barrier, inc=1, device_id={"span": span, "section": 1 - section},
        device_id_type=pl.DeviceIdType.MESH,
    )

    packed[...] = jnp.zeros_like(packed)
    packed_out[...] = jnp.zeros_like(packed_out)
    for part in range(2):
        for third in range(3):
            at = third * width + part * half_width
            to = third * half_width
            packed[part, 0:kept, to : to + half_width] = qkv_ref[:, at : at + half_width]

    pl.semaphore_wait(barrier, chips + 1)

    give = remote(packed.at[1 - core], got, pair_send.at[0], pair_recv.at[0], pair, section)
    give.start()
    for part in range(2):
        packed_out[part, 0:kept, 0:half_width] = out_w_ref[
            :, part * half_width : (part + 1) * half_width
        ]
    give_out = remote(packed_out.at[1 - core], got_out, pair_send.at[5], pair_recv.at[5], pair, section)
    give_out.start()
    give_frames = remote(frames.at[core], frames.at[core], pair_send.at[1], pair_recv.at[1], pair, section)
    give_frames.start()

    here = pl.ds(chip, 1)
    pieces = (held_a, held_b, held_out)
    for piece_ref in pieces:
        piece_ref[here, 2 * kept : block_rows, :] = jnp.zeros(
            (1, block_rows - 2 * kept, piece_ref.shape[2]), bf16
        )
    give.wait_recv()
    for which in range(2):

        @pl.when(core == which)
        def _():
            a, b = slice(which * kept, (which + 1) * kept), slice((1 - which) * kept, (2 - which) * kept)
            held_a[here, a, :] = packed[which, 0:kept, 0:cut_at][None]
            held_a[here, b, :] = got[0:kept, 0:cut_at][None]
            held_b[here, a, :] = packed[which, 0:kept, cut_at:][None]
            held_b[here, b, :] = got[0:kept, cut_at:][None]

    def forward(piece, lane, block, target):
        return remote(
            pieces[piece].at[block], pieces[piece].at[block],
            gather_send.at[piece * 3 + lane, block], gather_recv.at[piece, block],
            target, section,
        )

    def pass_on(piece, step):
        if step == 0:

            @pl.when(z_at < z_count - 1)
            def _():
                forward(piece, 0, chip, span + 4).start()

            @pl.when(z_at > 0)
            def _():
                forward(piece, 1, chip, span - 4).start()

            forward(piece, 2, chip, x_near).start()
        else:
            below = (z_at - step) * 2 + x_at
            above = (z_at + step) * 2 + x_at

            @pl.when(z_at >= step)
            def _():
                forward(piece, 2, below, x_near).wait_recv()

                @pl.when(z_at < z_count - 1)
                def _():
                    forward(piece, 0, below, span + 4).start()

                forward(piece, 2, below, x_near).start()

            @pl.when(z_at + step < z_count)
            def _():
                forward(piece, 2, above, x_near).wait_recv()

                @pl.when(z_at > 0)
                def _():
                    forward(piece, 1, above, span - 4).start()

                forward(piece, 2, above, x_near).start()

    def last_arrivals(piece):
        for z_from in range(z_count):
            forward(piece, 2, z_from * 2 + (1 - x_at), x_near).wait_recv()

    pass_on(0, 0)
    pass_on(1, 0)

    give_out.wait_recv()
    for which in range(2):

        @pl.when(core == which)
        def _():
            a, b = slice(which * kept, (which + 1) * kept), slice((1 - which) * kept, (2 - which) * kept)
            held_out[here, a, :] = packed_out[which, 0:kept, :][None]
            held_out[here, b, :] = got_out[0:kept, :][None]

    block_lanes = normed.shape[2]
    to_blocks[...] = spread(half_lanes, block_lanes, half_lanes, half_width, block_rows, 2 * kept)
    from_heads[...] = spread(heads * LANES, block_lanes, LANES, HEAD, block_rows, 2 * kept)
    window_at = [third * half_width // LANES * LANES for third in range(3)]
    for third in range(3):
        to_heads[third] = spread(
            window, heads * LANES, window, half_width, LANES, HEAD, third * half_width - window_at[third]
        )
    norm_scale[...] = jnp.zeros_like(norm_scale)
    for part in range(2):
        norm_scale[part : part + 1, 0:half_width] = norm_ref[
            :, part * half_width : (part + 1) * half_width
        ]
    head_scale[...] = jnp.zeros_like(head_scale)
    for head in range(2 * heads):
        head_scale[head : head + 1, 0:HEAD] = head_ref[:, head * HEAD : (head + 1) * HEAD]
    give_frames.wait()
    eye = lax.broadcasted_iota(jnp.int32, (padded, padded), 0) == lax.broadcasted_iota(
        jnp.int32, (padded, padded), 1
    )
    for which in range(2):
        along = jnp.broadcast_to(frames[which, 0:1, 0:padded], (padded, padded))
        down = jnp.sum(jnp.where(eye, along, 0.0), axis=1, keepdims=True)
        masks[which] = jnp.where(along <= down, 1.0, 0.0)

    mine = pl.ds(pl.multiple_of(core * padded, 16), padded)
    theirs = pl.ds(pl.multiple_of((1 - core) * padded, 16), padded)

    @pl.when(section == 0)
    def _():
        fresh[...] = jnp.zeros_like(fresh)
        for part in range(2):
            fresh[part, 0:rows, 0:half_width] = x_ref[
                :, part * half_width : (part + 1) * half_width
            ]
        put = pltpu.make_async_copy(fresh, stream.at[:, mine, :], local_sem)
        put.start()
        share = remote(fresh, stream.at[:, mine, :], pair_send.at[2], pair_recv.at[2], pair, section)
        share.start()
        put.wait()
        share.wait()

    for step in range(1, z_count):
        pass_on(0, step)
        pass_on(1, step)
    pass_on(2, 0)
    last_arrivals(0)
    last_arrivals(1)

    @pl.when(section == 1)
    def _():
        for step in range(1, z_count):
            pass_on(2, step)
        shares = []
        for chunk in range(2):
            at = stream.at[core, chunk * padded : (chunk + 1) * padded, :]
            remote(at, at, y_send.at[chunk], y_recv.at[chunk], span, 1 - section).wait_recv()
            slot = 2 + 4 * chunk
            share = remote(at, at, pair_send.at[slot], pair_recv.at[slot], pair, section)
            share.start()
            shares.append(share)
        for share in shares:
            share.wait()

    wide = [stream[part].astype(f32) for part in range(2)]
    square = sum(jnp.sum(value * value, axis=1, keepdims=True) for value in wide)
    inverse = lax.rsqrt(square / width + EPS)
    for part in range(2):
        scaled = (wide[part] * inverse * norm_scale[part : part + 1, :]).astype(bf16)
        normed[part] = jnp.dot(scaled, to_blocks[...], preferred_element_type=f32).astype(bf16)
    lanes = heads * LANES
    half_chips = chips // 2

    def weight_of(ref, part):
        block = ref[part * half_chips : (part + 1) * half_chips]
        return block.reshape(half_chips * block_rows, ref.shape[2])

    for index, ref in enumerate((held_a, held_b)):
        projected[:, index * cut_at : (index + 1) * cut_at] = (
            jnp.dot(normed[0], weight_of(ref, 0), preferred_element_type=f32)
            + jnp.dot(normed[1], weight_of(ref, 1), preferred_element_type=f32)
        ).astype(bf16)
    for third, into in ((1, keys), (2, values), (0, queries)):
        result = jnp.dot(
            projected[:, window_at[third] : window_at[third] + window], to_heads[third],
            preferred_element_type=f32,
        )
        into[...] = (result if third == 2 else jnp.maximum(result, 0.0)).astype(bf16)

    def pass_out(step):
        @pl.when(section == 0)
        def _():
            pass_on(2, step)

    pass_out(1)

    contract_rows = (((0,), (0,)), ((), ()))
    for which in range(2):
        at = slice(which * padded, (which + 1) * padded)
        for head in range(heads):
            cols = slice(head * LANES, (head + 1) * LANES)
            state[which, cols, :] = lax.dot_general(
                keys[at, cols], values[at, cols], contract_rows, preferred_element_type=f32
            )
    piece = sent_state.shape[1]
    sent_state[...] = (state[0] + state[1]).astype(bf16).reshape(chips, piece, LANES)

    def exchange(source, target, sends, recvs, step):
        other = (chip + step) % chips
        return remote(
            source.at[other], target.at[chip], sends.at[other], recvs.at[chip],
            other * 2 + core, section,
        )

    def landed(target, sends, recvs, step):
        other = (chip + step) % chips
        return remote(
            target.at[other], target.at[other], sends.at[other], recvs.at[other],
            other * 2 + core, section,
        )

    for step in range(1, chips):
        exchange(sent_state, got_state, state_send, state_recv, step).start()
    got_state[pl.ds(chip, 1)] = sent_state[pl.ds(chip, 1)]

    contract_lanes = (((1,), (1,)), ((), ()))

    def local_part(which):
        at = slice(which * padded, (which + 1) * padded)
        for head in range(heads):
            cols = slice(head * LANES, (head + 1) * LANES)
            scores = lax.dot_general(
                queries[at, cols], keys[at, cols], contract_lanes, preferred_element_type=f32
            )
            scores = jnp.where(masks[which] > 0.5, scores, 0.0).astype(bf16)
            mixed[at, cols] = jnp.dot(scores, values[at, cols], preferred_element_type=f32)

    local_part(0)
    pass_out(2)
    for step in range(1, chips):
        landed(got_state, state_send, state_recv, step).wait_recv()
    running = jnp.zeros((piece, LANES), f32)
    for index in range(chips):
        sent_sum[index] = running.astype(bf16)
        running = running + got_state[index].astype(f32)
    for step in range(1, chips):
        exchange(sent_sum, got_sum, sum_send, sum_recv, step).start()
    got_sum[pl.ds(chip, 1)] = sent_sum[pl.ds(chip, 1)]
    local_part(1)
    pass_out(3)
    for step in range(1, chips):
        landed(got_sum, sum_send, sum_recv, step).wait_recv()

    carried = got_sum[...].reshape(lanes, LANES)
    for which in range(2):
        at = slice(which * padded, (which + 1) * padded)
        for head in range(heads):
            cols = slice(head * LANES, (head + 1) * LANES)
            earlier = carried[cols, :]
            if which == 1:
                earlier = (earlier.astype(f32) + state[0, cols, :]).astype(bf16)
            mixture = mixed[at, cols] + jnp.dot(
                queries[at, cols], earlier, preferred_element_type=f32
            )
            size = jnp.sum(mixture * mixture, axis=1, keepdims=True) / HEAD
            queries[at, cols] = (
                mixture * lax.rsqrt(size + EPS) * head_scale[pl.ds(core * heads + head, 1), :]
            ).astype(bf16)
    fresh_heads = jnp.dot(queries[...], from_heads[...], preferred_element_type=f32)
    attended[pl.ds(core, 1)] = fresh_heads.astype(bf16)[None]
    swap = remote(attended.at[core], attended.at[core], pair_send.at[3], pair_recv.at[3], pair, section)
    swap.start()
    swap.wait()

    last_arrivals(2)

    def next_layer(chunk):
        at = slice(chunk * padded, (chunk + 1) * padded)
        return remote(
            keys.at[at, :], stream.at[core, at, :], y_send.at[chunk], y_recv.at[chunk],
            span, 1 - section,
        )

    for chunk in range(2):
        at = slice(chunk * padded, (chunk + 1) * padded)
        total = stream[pl.ds(core, 1), at, :].astype(f32)[0]
        for part in range(2):
            total = total + jnp.dot(
                attended[part, at, :], weight_of(held_out, part), preferred_element_type=f32
            )
        keys[at, :] = total.astype(bf16)

        @pl.when(section == 0)
        def _():
            next_layer(chunk).start()

    back = remote(keys.at[theirs, :], y_ref.at[core], pair_send.at[4], pair_recv.at[4], pair, section)
    back.start()
    keep = pltpu.make_async_copy(keys.at[mine, :], y_ref.at[core], local_sem)
    keep.start()
    keep.wait()
    back.wait()

    @pl.when(section == 0)
    def _():
        next_layer(0).wait_send()
        next_layer(1).wait_send()

    give.wait_send()
    for step in range(1, chips):
        exchange(sent_state, got_state, state_send, state_recv, step).wait_send()
        exchange(sent_sum, got_sum, sum_send, sum_recv, step).wait_send()
    give_out.wait_send()
    for piece in range(3):
        for z_from in range(z_count):
            block = z_from * 2 + x_at
            forward(piece, 2, block, x_near).wait_send()

            @pl.when((z_from <= z_at) & (z_at < z_count - 1))
            def _():
                forward(piece, 0, block, span + 4).wait_send()

            @pl.when((z_from >= z_at) & (z_at > 0))
            def _():
                forward(piece, 1, block, span - 4).wait_send()


def fused(clip_tokens, frame_ids, norm_gain, qkv_weight, head_gain, out_weight):
    shards = lax.axis_size("span")
    rows, width = clip_tokens.shape
    half_width = width // 2
    kept = width // shards
    heads = half_width // HEAD
    shard_rows = whole_tiles(kept, 16)
    padded = whole_tiles(rows, 16)
    half_lanes = whole_tiles(half_width, LANES)
    lanes = heads * LANES
    chips = shards // 2
    block_rows = whole_tiles(2 * kept, 16)
    block_lanes = chips // 2 * block_rows
    cut_at = whole_tiles(3 * half_width, 2 * LANES) // 2
    window = half_lanes + LANES
    bf16, f32 = jnp.bfloat16, jnp.float32
    dma = pltpu.SemaphoreType.DMA
    vmem = pl.BlockSpec(memory_space=pltpu.VMEM)
    y = pl.pallas_call(
        layers_kernel,
        out_shape=jax.ShapeDtypeStruct((2, padded, half_lanes), bf16),
        in_specs=[vmem] * 6,
        out_specs=vmem,
        scratch_shapes=[
            pltpu.VMEM((chips, block_rows, cut_at), bf16),
            pltpu.VMEM((chips, block_rows, cut_at), bf16),
            pltpu.VMEM((chips, block_rows, half_lanes), bf16),
            pltpu.VMEM((2, shard_rows, 2 * cut_at), bf16),
            pltpu.VMEM((2, shard_rows, half_lanes), bf16),
            pltpu.VMEM((shard_rows, 2 * cut_at), bf16),
            pltpu.VMEM((shard_rows, half_lanes), bf16),
            pltpu.VMEM((2, 2 * padded, half_lanes), bf16),
            pltpu.VMEM((2, 2 * padded, block_lanes), bf16),
            pltpu.VMEM((2 * padded, 2 * cut_at), bf16),
            pltpu.VMEM((2 * padded, lanes), bf16),
            pltpu.VMEM((2 * padded, lanes), bf16),
            pltpu.VMEM((2 * padded, lanes), bf16),
            pltpu.VMEM((2 * padded, lanes), f32),
            pltpu.VMEM((2, 2 * padded, block_lanes), bf16),
            pltpu.VMEM((2, padded, half_lanes), bf16),
            pltpu.VMEM((2, lanes, LANES), f32),
            pltpu.VMEM((chips, lanes // chips, LANES), bf16),
            pltpu.VMEM((chips, lanes // chips, LANES), bf16),
            pltpu.VMEM((chips, lanes // chips, LANES), bf16),
            pltpu.VMEM((chips, lanes // chips, LANES), bf16),
            pltpu.VMEM((2, 8, whole_tiles(padded, LANES)), f32),
            pltpu.VMEM((2, padded, padded), f32),
            pltpu.VMEM((8, half_lanes), f32),
            pltpu.VMEM((whole_tiles(2 * heads, 8), LANES), f32),
            pltpu.VMEM((half_lanes, block_lanes), bf16),
            pltpu.VMEM((lanes, block_lanes), bf16),
            pltpu.VMEM((3, window, lanes), bf16),
            dma((9, chips)),
            dma((3, chips)),
            dma((7,)),
            dma((7,)),
            dma((chips,)),
            dma((chips,)),
            dma((chips,)),
            dma((chips,)),
            dma((2,)),
            dma((2,)),
            dma,
        ],
        compiler_params=pltpu.CompilerParams(
            collective_id=0, has_side_effects=True, vmem_limit_bytes=48 * 1024 * 1024
        ),
    )(
        clip_tokens,
        frame_ids.reshape(1, rows),
        norm_gain,
        qkv_weight.reshape(kept, -1),
        head_gain,
        out_weight.reshape(kept, width),
    )
    halves = y[:, :rows, :half_width]
    return jnp.concatenate([halves[0], halves[1]], axis=1)[None]


def grid_fits(mesh):
    return mesh.shape["span"] == 16 and mesh.shape["section"] == 2


def solution(mesh):
    return jax.shard_map(
        fused if grid_fits(mesh) else on_device,
        mesh=mesh,
        in_specs=(
            P("span", None),
            P("span"),
            P("section", None),
            P("section", "span"),
            P("section", None),
            P("section", "span"),
        ),
        out_specs=P("section", "span", None),
        check_vma=False,
    )
```
